32 devices in a mesh: slab: 4 (over z), member: 8 (over y, x, core).
Axes of the slice: x: 2, y: 2, z: 4, core: 2. Of those that a mesh axis runs over, the one named last changes fastest.
Arguments:
- state: float32 [16, 64, 4096], P('member', 'slab'), may hold values from -6 to 6
- winds: float32 [2, 64, 4096], P(None, 'slab'), may hold values from -0.35 to 0.35
- kappa: float32 [64, 4096], P('slab'), may hold values from 0.05 to 0.22
- obs_values: float32 [512, 128], P('slab'), may hold values from -6 to 6
- obs_rinv: float32 [512, 128], P('slab'), may hold values from 0.1 to 1
- owner: int32 [512, 1], P('slab'), may hold values from 0 to 3; in each aligned block of 128 rows (0 to 127, 128 to 255, ...) at most 64 rows name the same one
- obs_rows: int32 [512], P('slab'), may hold values from 0 to 15
- obs_tiles: int32 [512], P('slab'), may hold values from 0 to 31
- counts: int32 [4], P('slab'), may hold values from 64 to 128, as said below
- tile_mask: int32 [4, 32, 32], P('slab'), may hold values 0 or 1
Outputs:
- analysis: float32 [16, 64, 4096], P('member', 'slab')
The draws below stay inside these ranges and needn't reach their ends.
Inputs may be any that keep to these rules, and one draw needn't show every extreme that they name: Among the 128 profile rows of one slab index at most 64 name the same owner, a bound that some block reaches of them. `counts`: some slab index has all 128 rows live.
All inputs are finite; a program needn't handle non-finite values. No bound on the sum of `tile_mask` on one device may be relied on, other than what follows from the above.
Results may differ from the reference program's by a relative error of at most 0.00011.
Values sent between devices are 32-bit elements; how exact they have to be, the bound alone decides.
A program may use at most 64 MiB of HBM per device.

```python
import math
import jax
import jax.numpy as jnp
import numpy as np
from jax import lax

LON = 4096
PROF = 128
LAT_DEV = 16
PRO_DEV = 128
FSTEPS = 2
NS_ITERS = 6
ENS = 16
SLABS = 4
LAT = 64
NTILE = 32
PROFILES = 512
CAP = 64
N_SLAB = 4


def draw_counts(key, part):
    key_base, key_order = jax.random.split(jax.random.fold_in(key, 11))
    base_counts = jax.random.randint(key_base, (SLABS,), PRO_DEV // 2, PRO_DEV + 1)
    ordering = jax.random.permutation(key_order, SLABS)
    base_counts = base_counts.at[ordering[0]].set(PRO_DEV)
    base_counts = base_counts.at[ordering[1]].set(PRO_DEV // 2)
    return base_counts.astype(jnp.int32)


def set_ends(values, own_key, smallest, largest):
    index_at = [jax.random.randint(jax.random.fold_in(own_key, axis), (), 0, length) for axis, length in enumerate(values.shape)]
    main_axis = values.shape.index(max(values.shape))
    neighbour = index_at[:main_axis] + [(index_at[main_axis] + 1) % values.shape[main_axis]] + index_at[main_axis + 1:]
    return values.at[tuple(index_at)].set(smallest).at[tuple(neighbour)].set(largest)


def steps_of(rng, extent, shards, smallest, high):
    def one(dim, parts):
        heights = jax.random.uniform(jax.random.fold_in(jax.random.fold_in(rng, 6), dim), (parts,), jnp.float32, smallest / len(shards), high / len(shards))
        return jnp.repeat(jnp.exp(heights), extent[dim] // parts).reshape((-1,) + (1,) * (len(extent) - dim - 1))

    gain = one(*shards[0])
    for cut in shards[1:]:
        gain = gain * one(*cut)
    return gain


def deal_out(own_key, own, number, rows, count, top, reach, skew):
    sequence = jax.random.permutation(own_key, count)
    packed, common = portions_of(count, rows * top, reach, skew, True), portions_of(count, rows * top, reach, skew, False)
    places = jnp.arange(count)

    def named(sizes, rotation):
        used = int((sizes > 0).sum())
        fixed = max(1, used // 4)
        shifted = fixed + (places - fixed + rotation * (used - fixed)) % max(1, count - fixed)
        return jnp.zeros((count,), jnp.int32).at[sequence[jnp.where(places < fixed, places, shifted)]].set(jnp.asarray(sizes, jnp.int32))

    sizes = jnp.where(number % 4 == 0, named(packed, number // 4), named(common, number - number // 4 - 1))
    mixed = jax.random.permutation(jax.random.fold_in(own, 3), count)
    donor, taker = mixed[0:count // 2 * 2:2], mixed[1:count // 2 * 2:2]
    margin = jnp.minimum(sizes[donor] - 1, reach - sizes[taker]) // 2
    margin = jnp.where((donor == sequence[0]) | (taker == sequence[0]) | (sizes[taker] == 0), 0, jnp.maximum(margin, 0))
    shifted = jax.random.randint(jax.random.fold_in(own, 4), (count // 2,), 0, 1 << 20) % (margin + 1)
    sizes = sizes.at[donor].add(-shifted).at[taker].add(shifted)
    items = jnp.searchsorted(jnp.cumsum(sizes), jnp.arange(rows * top), side="right").astype(jnp.int32)
    grid = items.reshape(top, rows).T
    grid = grid[jax.random.permutation(jax.random.fold_in(own, 1), rows)]
    rotation = jax.random.randint(jax.random.fold_in(own, 2), (rows, 1), 0, top)
    return jnp.take_along_axis(grid, (jnp.arange(top)[None, :] + rotation) % top, axis=1)


def portions_of(number_of, total, limit, lean, full):
    loads = [(1 << 20) // math.isqrt(grade ** lean) + 1 for grade in range(1, number_of + 1)]
    largest = limit if full else min(limit, max(-(-total // number_of), total * loads[0] // sum(loads)))
    least = 1 if total - largest >= number_of - 1 else 0
    given, spare = [largest] + [least] * (number_of - 1), total - largest - least * (number_of - 1)
    while spare > 0:
        free = [i for i in range(1, number_of) if given[i] < largest] or [i for i in range(1, number_of) if given[i] < limit]
        pool, remaining = sum([loads[i] for i in free]), spare
        for i in free:
            more = min(limit - given[i], max(1, remaining * loads[i] // pool), spare)
            given[i] = given[i] + more
            spare = spare - more
    return np.array(given)


def noise(own_key, dims, deviation, most, pieces=(), kind=jnp.bfloat16):
    values = jax.random.normal(own_key, dims, jnp.float32) * deviation
    if len(pieces) > 0:
        values = steps_of(own_key, dims, pieces, -0.22, 0.18) * values
    return jnp.clip(values, min=-most, max=most).astype(kind)


def setup_inputs(seed: int = 0) -> dict:
    streams_of = jax.random.split(jax.random.key(seed), 11)
    state = noise(streams_of[0], (ENS, LAT, LON), 1.0, 6.0, ((0, 8), (1, 4)), jnp.float32)
    winds = jnp.clip(jax.random.uniform(streams_of[1], (2, LAT, LON), jnp.float32, -0.35, 0.35) * steps_of(streams_of[1], (2, LAT, LON), ((1, 4),), -0.4, 0.0), -0.35, 0.35)
    kappa = jnp.clip(jnp.exp(math.log(0.22) - 1.48160452 * jax.random.uniform(streams_of[2], (LAT, LON), jnp.float32) ** steps_of(streams_of[2], (LAT, LON), ((0, 4),), -0.2, 0.2)), 0.05, 0.22)
    obs_values = noise(streams_of[3], (PROFILES, PROF), 1.0, 6.0, ((0, 4),), jnp.float32)
    obs_rinv = jnp.clip(jnp.exp(math.log(1.0) - 2.3025851 * jax.random.uniform(streams_of[4], (PROFILES, PROF), jnp.float32) ** steps_of(streams_of[4], (PROFILES, PROF), ((0, 4),), -0.2, 0.2)), 0.1, 1.0)
    owner_keys = jax.random.split(jax.random.fold_in(streams_of[5], 1), PROFILES // PRO_DEV)
    owner_turns = jax.random.permutation(jax.random.fold_in(streams_of[5], 3), PROFILES // PRO_DEV)
    owner = jax.vmap(lambda own, number: deal_out(jax.random.fold_in(streams_of[5], 2), own, number, PRO_DEV, N_SLAB, 1, CAP, 2))(owner_keys, owner_turns).reshape((PROFILES, 1))
    obs_rows = set_ends(jax.random.randint(streams_of[6], (PROFILES,), 0, LAT_DEV), jax.random.fold_in(streams_of[6], 1), 0, LAT_DEV - 1).astype(jnp.int32)
    obs_tiles = set_ends(jax.random.randint(streams_of[7], (PROFILES,), 0, NTILE), jax.random.fold_in(streams_of[7], 1), 0, NTILE - 1).astype(jnp.int32)
    counts = draw_counts(jax.random.fold_in(streams_of[10], 71), 0)
    tile_mask = set_ends((jax.random.randint(streams_of[9], (SLABS, NTILE, NTILE), 0, 2) < 1).astype(jnp.int32), jax.random.fold_in(streams_of[9], 1), 0, 1)
    return dict(state=state, winds=winds, kappa=kappa, obs_values=obs_values, obs_rinv=obs_rinv, owner=owner, obs_rows=obs_rows, obs_tiles=obs_tiles, counts=counts, tile_mask=tile_mask)


HIGHEST_PRECISION = lax.Precision.HIGHEST

def step_forward(predict_members, winds, kappa):
    bordered_field = jnp.pad(predict_members, ((0, 0), (1, 1), (0, 0)))
    northern_row = bordered_field[:, 2:]
    southern_row = bordered_field[:, :-2]
    eastern_column = jnp.roll(predict_members, -1, 2)
    western_column = jnp.roll(predict_members, 1, 2)
    return predict_members - winds[0] * (eastern_column - western_column) * 0.5 - winds[1] * (northern_row - southern_row) * 0.5 + kappa * (eastern_column + western_column + northern_row + southern_row - 4.0 * predict_members)

def inverse_root(matrix, order_size):
    identity = jnp.eye(order_size, dtype=jnp.float32)
    frob_norm = jnp.sqrt(lax.optimization_barrier(jnp.sum(matrix * matrix, axis=(-2, -1), keepdims=True)) + 1e-06)
    iterate = matrix / frob_norm
    factor = jnp.broadcast_to(identity, matrix.shape)
    for step_number in range(NS_ITERS):
        middle = 1.5 * identity - 0.5 * jnp.matmul(factor, iterate, precision=HIGHEST_PRECISION)
        iterate = jnp.matmul(iterate, middle, precision=HIGHEST_PRECISION)
        factor = jnp.matmul(middle, factor, precision=HIGHEST_PRECISION)
    return factor / jnp.sqrt(frob_norm)

def weights_for(gram_total, innov_total, members):
    identity = jnp.eye(members, dtype=jnp.float32)
    inv_root = inverse_root(gram_total + (members - 1.0) * identity, members)
    half_step = jnp.einsum('...ij,...j->...i', inv_root, innov_total, precision=HIGHEST_PRECISION)
    mean_shift = jnp.einsum('...ij,...j->...i', inv_root, half_step, precision=HIGHEST_PRECISION)
    return mean_shift[..., :, None] + math.sqrt(members - 1.0) * inv_root

def reference(state, winds, kappa, obs_values, obs_rinv, owner, obs_rows, obs_tiles, counts, tile_mask):
    predict_members = state
    for step_number in range(FSTEPS):
        predict_members = step_forward(predict_members, winds, kappa)
    ensemble_average = lax.optimization_barrier(jnp.mean(predict_members, axis=0))
    member_deviation = predict_members - ensemble_average
    anomaly_tiles = member_deviation.reshape(ENS, LAT, NTILE, PROF)
    owners = owner[:, 0]
    grid_rows = owners * LAT_DEV + obs_rows
    position = jnp.arange(PROFILES, dtype=jnp.int32)
    is_live = position % PRO_DEV < counts[position // PRO_DEV]
    observed = anomaly_tiles[:, grid_rows, obs_tiles]
    mean_seen = ensemble_average.reshape(LAT, NTILE, PROF)[grid_rows, obs_tiles]
    weights = obs_rinv * is_live[:, None].astype(jnp.float32)
    profile_grams = jnp.einsum('iph,ph,jph->pij', observed, weights, observed, precision=HIGHEST_PRECISION)
    innovation = jnp.einsum('iph,ph->pi', observed, weights * (obs_values - mean_seen), precision=HIGHEST_PRECISION)
    segment_ids = (owners * NTILE + obs_tiles).astype(jnp.int32)
    gram_part = jax.ops.segment_sum(profile_grams, segment_ids, num_segments=SLABS * NTILE).reshape(SLABS, NTILE, ENS, ENS)
    innov_part = jax.ops.segment_sum(innovation, segment_ids, num_segments=SLABS * NTILE).reshape(SLABS, NTILE, ENS)
    tile_use = jnp.maximum(tile_mask.astype(jnp.float32), jnp.eye(NTILE, dtype=jnp.float32))
    gram_sum = jnp.einsum('ots,osij->otij', tile_use, gram_part, precision=HIGHEST_PRECISION)
    innov_sum = jnp.einsum('ots,osi->oti', tile_use, innov_part, precision=HIGHEST_PRECISION)
    mixing = weights_for(gram_sum, innov_sum, ENS)
    blocks = member_deviation.reshape(ENS, SLABS, LAT_DEV, NTILE, PROF)
    update = jnp.einsum('iorth,otij->jorth', blocks, mixing, precision=HIGHEST_PRECISION)
    update = update + ensemble_average.reshape(SLABS, LAT_DEV, NTILE, PROF)
    return update.reshape(ENS, LAT, LON)
```

```python
import math

import jax
import jax.numpy as jnp
from jax import lax
from jax.sharding import PartitionSpec as P

PROF = 128
FSTEPS = 2
NS_ITERS = 6


HIGHEST_PRECISION = lax.Precision.HIGHEST


def padded(cells, sides, width):
    for axis, dim in sides:
        count = lax.axis_size(axis)
        ends = count - 1
        head = lax.slice_in_dim(cells, 0, width, axis=dim)
        tail = lax.slice_in_dim(cells, cells.shape[dim] - width, cells.shape[dim], axis=dim)
        cells = jnp.concatenate(
            [
                lax.ppermute(tail, axis, [(i, (i + 1) % count) for i in range(ends)]),
                cells,
                lax.ppermute(head, axis, [((i + 1) % count, i) for i in range(ends)]),
            ],
            axis=dim,
        )
    return cells


def step_forward_border(widened_field, coeff_east, coeff_north, diffusion):
    middle_row = widened_field[:, 1:-1]
    northern_row = widened_field[:, 2:]
    southern_row = widened_field[:, :-2]
    eastern_column = jnp.roll(middle_row, -1, 2)
    western_column = jnp.roll(middle_row, 1, 2)
    return (
        middle_row
        - coeff_east * (eastern_column - western_column) * 0.5
        - coeff_north * (northern_row - southern_row) * 0.5
        + diffusion
        * (eastern_column + western_column + northern_row + southern_row - 4.0 * middle_row)
    )


def inverse_root(matrix, order_size):
    identity = jnp.eye(order_size, dtype=jnp.float32)
    frob_norm = jnp.sqrt(jnp.sum(matrix * matrix, axis=(-2, -1), keepdims=True) + 1e-06)
    iterate = matrix / frob_norm
    factor = jnp.broadcast_to(identity, matrix.shape)
    for step_number in range(NS_ITERS):
        middle = 1.5 * identity - 0.5 * jnp.matmul(factor, iterate, precision=HIGHEST_PRECISION)
        iterate = jnp.matmul(iterate, middle, precision=HIGHEST_PRECISION)
        factor = jnp.matmul(middle, factor, precision=HIGHEST_PRECISION)
    return factor / jnp.sqrt(frob_norm)


def weights_for(gram_total, innov_total, members):
    identity = jnp.eye(members, dtype=jnp.float32)
    inv_root = inverse_root(gram_total + (members - 1.0) * identity, members)
    half_step = jnp.einsum("...ij,...j->...i", inv_root, innov_total, precision=HIGHEST_PRECISION)
    mean_shift = jnp.einsum("...ij,...j->...i", inv_root, half_step, precision=HIGHEST_PRECISION)
    return mean_shift[..., :, None] + math.sqrt(members - 1.0) * inv_root


def on_device(
    state, winds, kappa, obs_values, obs_rinv, owner, obs_rows, obs_tiles, counts, tile_mask
):
    lat_rows = state.shape[1]
    predict_members = state
    for step_number in range(FSTEPS):
        widened_field = padded(predict_members, (("slab", 1),), 1)
        predict_members = step_forward_border(widened_field, winds[0], winds[1], kappa)
    cell_major_layout = lax.all_to_all(
        predict_members, "member", split_axis=2, concat_axis=0, tiled=True
    )
    ensemble = cell_major_layout.shape[0]
    cell_width = cell_major_layout.shape[2]
    tiles_here = cell_width // PROF
    ensemble_average = jnp.mean(cell_major_layout, axis=0)
    member_deviation = cell_major_layout - ensemble_average
    slab_count = lax.axis_size("slab")
    per_slab = owner.shape[0]
    first_tile = lax.axis_index("member") * tiles_here
    cells = lat_rows * tiles_here
    tile_off = obs_tiles - first_tile
    inside = (
        (tile_off >= 0)
        & (tile_off < tiles_here)
        & (jnp.arange(per_slab, dtype=jnp.int32) < counts[0])
    )
    target = jnp.where(
        inside, owner[:, 0] * cells + obs_rows * tiles_here + tile_off, -1
    )
    placing = (
        target[None, :] == jnp.arange(slab_count * cells, dtype=jnp.int32)[:, None]
    ).astype(jnp.float32)
    payload = jnp.concatenate([obs_rinv, obs_rinv * obs_values], axis=1)
    sums = jnp.matmul(placing, payload, precision=HIGHEST_PRECISION)
    sums = lax.all_to_all(
        sums.reshape(slab_count, lat_rows, tiles_here, 2, PROF),
        "slab",
        split_axis=0,
        concat_axis=0,
        tiled=True,
    )
    sums = jnp.sum(sums, axis=0)
    cell_weight, cell_value = sums[:, :, 0], sums[:, :, 1]
    blocks = member_deviation.reshape(ensemble, lat_rows, tiles_here, PROF)
    mean_blocks = ensemble_average.reshape(lat_rows, tiles_here, PROF)
    gram_here = jnp.einsum(
        "irth,jrth->tij", blocks * cell_weight, blocks, precision=HIGHEST_PRECISION
    )
    innov_here = jnp.einsum(
        "irth,rth->ti",
        blocks,
        cell_value - cell_weight * mean_blocks,
        precision=HIGHEST_PRECISION,
    )
    tile_count = tile_mask.shape[1]
    tile_use = jnp.maximum(tile_mask[0].astype(jnp.float32), jnp.eye(tile_count, dtype=jnp.float32))
    use_mine = lax.dynamic_slice_in_dim(tile_use, first_tile, tiles_here, 0)
    gram_next = jnp.einsum(
        "ts,sij->tij",
        use_mine,
        lax.all_gather(gram_here, "member", axis=0, tiled=True),
        precision=HIGHEST_PRECISION,
    )
    innov_next = jnp.einsum(
        "ts,si->ti",
        use_mine,
        lax.all_gather(innov_here, "member", axis=0, tiled=True),
        precision=HIGHEST_PRECISION,
    )
    mixing = weights_for(gram_next, innov_next, ensemble)
    update = jnp.einsum("irth,tij->jrth", blocks, mixing, precision=HIGHEST_PRECISION)
    update = update + ensemble_average.reshape(lat_rows, tiles_here, PROF)
    return lax.all_to_all(
        update.reshape(ensemble, lat_rows, cell_width),
        "member",
        split_axis=0,
        concat_axis=2,
        tiled=True,
    )


def solution(mesh):
    placed = (
        P("member", "slab", None),
        P(None, "slab", None),
        P("slab", None),
        P("slab", None),
        P("slab", None),
        P("slab", None),
        P("slab"),
        P("slab"),
        P("slab"),
        P("slab", None, None),
    )
    return jax.shard_map(
        on_device, mesh=mesh, in_specs=placed, out_specs=P("member", "slab", None), check_vma=False
    )
```

```python
import functools
import math

import jax
import jax.numpy as jnp
from jax import lax
from jax.experimental import pallas as pl
from jax.experimental.pallas import tpu as pltpu
from jax.sharding import PartitionSpec as P

PROF = 128
FSTEPS = 2
NS_ITERS = 6


HIGHEST_PRECISION = lax.Precision.HIGHEST


def padded(cells, sides, width):
    for axis, dim in sides:
        count = lax.axis_size(axis)
        ends = count - 1
        head = lax.slice_in_dim(cells, 0, width, axis=dim)
        tail = lax.slice_in_dim(cells, cells.shape[dim] - width, cells.shape[dim], axis=dim)
        cells = jnp.concatenate(
            [
                lax.ppermute(tail, axis, [(i, (i + 1) % count) for i in range(ends)]),
                cells,
                lax.ppermute(head, axis, [((i + 1) % count, i) for i in range(ends)]),
            ],
            axis=dim,
        )
    return cells


def step_forward_border(widened_field, coeff_east, coeff_north, diffusion):
    middle_row = widened_field[:, 1:-1]
    northern_row = widened_field[:, 2:]
    southern_row = widened_field[:, :-2]
    eastern_column = jnp.roll(middle_row, -1, 2)
    western_column = jnp.roll(middle_row, 1, 2)
    return (
        middle_row
        - coeff_east * (eastern_column - western_column) * 0.5
        - coeff_north * (northern_row - southern_row) * 0.5
        + diffusion
        * (eastern_column + western_column + northern_row + southern_row - 4.0 * middle_row)
    )


def inverse_root(matrix, order_size):
    identity = jnp.eye(order_size, dtype=jnp.float32)
    frob_norm = jnp.sqrt(jnp.sum(matrix * matrix, axis=(-2, -1), keepdims=True) + 1e-06)
    iterate = matrix / frob_norm
    factor = jnp.broadcast_to(identity, matrix.shape)
    for step_number in range(NS_ITERS):
        middle = 1.5 * identity - 0.5 * jnp.matmul(factor, iterate, precision=HIGHEST_PRECISION)
        iterate = jnp.matmul(iterate, middle, precision=HIGHEST_PRECISION)
        factor = jnp.matmul(middle, factor, precision=HIGHEST_PRECISION)
    return factor / jnp.sqrt(frob_norm)


def weights_for(gram_total, innov_total, members):
    identity = jnp.eye(members, dtype=jnp.float32)
    inv_root = inverse_root(gram_total + (members - 1.0) * identity, members)
    half_step = jnp.einsum("...ij,...j->...i", inv_root, innov_total, precision=HIGHEST_PRECISION)
    mean_shift = jnp.einsum("...ij,...j->...i", inv_root, half_step, precision=HIGHEST_PRECISION)
    return mean_shift[..., :, None] + math.sqrt(members - 1.0) * inv_root


def on_device(
    state, winds, kappa, obs_values, obs_rinv, owner, obs_rows, obs_tiles, counts, tile_mask
):
    lat_rows = state.shape[1]
    predict_members = state
    for step_number in range(FSTEPS):
        widened_field = padded(predict_members, (("slab", 1),), 1)
        predict_members = step_forward_border(widened_field, winds[0], winds[1], kappa)
    cell_major_layout = lax.all_to_all(
        predict_members, "member", split_axis=2, concat_axis=0, tiled=True
    )
    ensemble = cell_major_layout.shape[0]
    cell_width = cell_major_layout.shape[2]
    tiles_here = cell_width // PROF
    ensemble_average = jnp.mean(cell_major_layout, axis=0)
    member_deviation = cell_major_layout - ensemble_average
    slab_count = lax.axis_size("slab")
    per_slab = owner.shape[0]
    first_tile = lax.axis_index("member") * tiles_here
    cells = lat_rows * tiles_here
    tile_off = obs_tiles - first_tile
    inside = (
        (tile_off >= 0)
        & (tile_off < tiles_here)
        & (jnp.arange(per_slab, dtype=jnp.int32) < counts[0])
    )
    target = jnp.where(
        inside, owner[:, 0] * cells + obs_rows * tiles_here + tile_off, -1
    )
    placing = (
        target[None, :] == jnp.arange(slab_count * cells, dtype=jnp.int32)[:, None]
    ).astype(jnp.float32)
    payload = jnp.concatenate([obs_rinv, obs_rinv * obs_values], axis=1)
    sums = jnp.matmul(placing, payload, precision=HIGHEST_PRECISION)
    sums = lax.all_to_all(
        sums.reshape(slab_count, lat_rows, tiles_here, 2, PROF),
        "slab",
        split_axis=0,
        concat_axis=0,
        tiled=True,
    )
    sums = jnp.sum(sums, axis=0)
    cell_weight, cell_value = sums[:, :, 0], sums[:, :, 1]
    blocks = member_deviation.reshape(ensemble, lat_rows, tiles_here, PROF)
    mean_blocks = ensemble_average.reshape(lat_rows, tiles_here, PROF)
    gram_here = jnp.einsum(
        "irth,jrth->tij", blocks * cell_weight, blocks, precision=HIGHEST_PRECISION
    )
    innov_here = jnp.einsum(
        "irth,rth->ti",
        blocks,
        cell_value - cell_weight * mean_blocks,
        precision=HIGHEST_PRECISION,
    )
    tile_count = tile_mask.shape[1]
    tile_use = jnp.maximum(tile_mask[0].astype(jnp.float32), jnp.eye(tile_count, dtype=jnp.float32))
    use_mine = lax.dynamic_slice_in_dim(tile_use, first_tile, tiles_here, 0)
    gram_next = jnp.einsum(
        "ts,sij->tij",
        use_mine,
        lax.all_gather(gram_here, "member", axis=0, tiled=True),
        precision=HIGHEST_PRECISION,
    )
    innov_next = jnp.einsum(
        "ts,si->ti",
        use_mine,
        lax.all_gather(innov_here, "member", axis=0, tiled=True),
        precision=HIGHEST_PRECISION,
    )
    mixing = weights_for(gram_next, innov_next, ensemble)
    update = jnp.einsum("irth,tij->jrth", blocks, mixing, precision=HIGHEST_PRECISION)
    update = update + ensemble_average.reshape(lat_rows, tiles_here, PROF)
    return lax.all_to_all(
        update.reshape(ensemble, lat_rows, cell_width),
        "member",
        split_axis=0,
        concat_axis=2,
        tiled=True,
    )


def split3(x):
    high = x.astype(jnp.bfloat16)
    rest = x - high.astype(jnp.float32)
    middle = rest.astype(jnp.bfloat16)
    low = (rest - middle.astype(jnp.float32)).astype(jnp.bfloat16)
    return high, middle, low


def split2(x):
    high = x.astype(jnp.bfloat16)
    return high, (x - high.astype(jnp.float32)).astype(jnp.bfloat16)


def dot16(a, b, dims=((1,), (0,))):
    return lax.dot_general(a, b, (dims, ((), ())), preferred_element_type=jnp.float32)


def dot32(a, b, dims=((1,), (0,))):
    return lax.dot_general(
        a,
        b,
        (dims, ((), ())),
        precision=HIGHEST_PRECISION,
        preferred_element_type=jnp.float32,
    )


def iota(shape, dim):
    return lax.broadcasted_iota(jnp.int32, shape, dim)


def exact_rows(x, ones):
    rows = x.shape[0]
    whole = dot16(jnp.concatenate(split3(x), axis=0), ones)
    return whole[:rows] + whole[rows : 2 * rows] + whole[2 * rows :]


def kernel(
    slabs,
    group,
    state,
    winds,
    kappa,
    target,
    obs_values,
    obs_rinv,
    tile_mask,
    out,
    first,
    fields,
    edge_out,
    edge_in,
    obs_out,
    obs_in,
    seen,
    part,
    parts,
    dev_high,
    dev_low,
    weighted_high,
    weighted_low,
    innov_rows,
    mean_ref,
    gather_sel,
    use_sel,
    result,
    edge_send,
    edge_recv,
    obs_send,
    obs_recv,
    field_send,
    field_recv,
    part_send,
    part_recv,
    back_send,
    back_recv,
    own_sem,
):
    me_slab, me = lax.axis_index("slab"), lax.axis_index("member")
    held, rows, lon = state.shape
    width = lon // group
    tiles = width // PROF
    members = held * group
    span = members * rows
    lanes = part.shape[1]
    packed = tiles * members
    all_tiles = tile_mask.shape[1]

    def peer(k):
        return lax.rem(me + k, group)

    def source(k):
        return lax.rem(me + group - k, group)

    def peer_slab(k):
        return lax.rem(me_slab + k, slabs)

    def source_slab(k):
        return lax.rem(me_slab + slabs - k, slabs)

    def remote(src, dst, send, recv, slab, member):
        return pltpu.make_async_remote_copy(
            src_ref=src,
            dst_ref=dst,
            send_sem=send,
            recv_sem=recv,
            device_id=(slab, member),
            device_id_type=pl.DeviceIdType.MESH,
        )

    barrier = pltpu.get_barrier_semaphore()
    for k in range(1, group):
        pl.semaphore_signal(
            barrier, inc=1, device_id=(me_slab, peer(k)), device_id_type=pl.DeviceIdType.MESH
        )
    for k in range(1, slabs):
        pl.semaphore_signal(
            barrier, inc=1, device_id=(peer_slab(k), me), device_id_type=pl.DeviceIdType.MESH
        )

    cells = slabs * tiles * rows
    placing = (iota((cells, target.shape[1]), 0) == target[...]).astype(jnp.bfloat16)
    rinv = obs_rinv[...]
    payload = jnp.concatenate([rinv, rinv * obs_values[...]], axis=1)
    sums = sum(dot16(placing, piece) for piece in split3(payload))
    for o in range(slabs):
        for t in range(tiles):
            at = (o * tiles + t) * rows
            obs_out[o, 0, :, t * PROF : (t + 1) * PROF] = sums[at : at + rows, :PROF]
            obs_out[o, 1, :, t * PROF : (t + 1) * PROF] = sums[at : at + rows, PROF:]
    for m in range(held):
        edge_out[0, m : m + 1, :] = state[m, 0:1, :]
        edge_out[1, m : m + 1, :] = state[m, rows - 1 : rows, :]

    pl.semaphore_wait(barrier, group + slabs - 2)

    def edges(step, act):
        south, north = 2 * step, 2 * step + 1

        @pl.when(me_slab > 0)
        def _():
            act(south, north, me_slab - 1, 0)

        @pl.when(me_slab < slabs - 1)
        def _():
            act(north, south, me_slab + 1, 1)

    def edge_copy(mine, theirs, slab):
        return remote(
            edge_out.at[mine],
            edge_in.at[theirs],
            edge_send.at[mine],
            edge_recv.at[theirs],
            slab,
            me,
        )

    def edge_arrived(mine, slab):
        return remote(
            edge_out.at[mine],
            edge_in.at[mine],
            edge_send.at[mine],
            edge_recv.at[mine],
            slab,
            me,
        )

    def coefficients(row, side, at):
        sign = 0.5 if side == 0 else -0.5
        return sign * winds[1, row : row + 1, at] + kappa[row : row + 1, at]

    def advance(load, store):
        def body(c, carry):
            at = pl.multiple_of(c * width, PROF)
            before = pl.multiple_of(lax.rem(c * width + lon - PROF, lon), PROF)
            after = pl.multiple_of(lax.rem(c * width + width, lon), PROF)
            east_wind = 0.5 * winds[0, :, pl.ds(at, width)]
            north_wind = 0.5 * winds[1, :, pl.ds(at, width)]
            mix = kappa[:, pl.ds(at, width)]
            row = iota((rows, width), 0)
            for m in range(held):
                cell = load[m, :, pl.ds(at, width)]
                wide = jnp.concatenate(
                    [load[m, :, pl.ds(before, PROF)], cell, load[m, :, pl.ds(after, PROF)]], axis=1
                )
                east = pltpu.roll(wide, width + 2 * PROF - 1, 1)[:, PROF : PROF + width]
                west = pltpu.roll(wide, 1, 1)[:, PROF : PROF + width]
                north = jnp.where(row == rows - 1, 0.0, pltpu.roll(cell, rows - 1, 0))
                south = jnp.where(row == 0, 0.0, pltpu.roll(cell, 1, 0))
                store(
                    c,
                    at,
                    m,
                    cell
                    - east_wind * (east - west)
                    - north_wind * (north - south)
                    + mix * (east + west + north + south - 4.0 * cell),
                )
            return carry

        lax.fori_loop(0, group, body, 0)

    edges(0, lambda mine, theirs, slab, side: edge_copy(mine, theirs, slab).start())

    def store_first(c, at, m, value):
        first[m, :, pl.ds(at, width)] = value

    advance(state, store_first)

    def mend_first(mine, theirs, slab, side):
        edge_arrived(mine, slab).wait_recv()
        row = 0 if side == 0 else rows - 1
        gain = coefficients(row, side, slice(None))
        for m in range(held):
            first[m, row : row + 1, :] += gain * edge_in[mine, m : m + 1, :]

    edges(0, mend_first)
    for m in range(held):
        edge_out[2, m : m + 1, :] = first[m, 0:1, :]
        edge_out[3, m : m + 1, :] = first[m, rows - 1 : rows, :]
    edges(1, lambda mine, theirs, slab, side: edge_copy(mine, theirs, slab).start())

    def obs_copy(k):
        return remote(
            obs_out.at[peer_slab(k)],
            obs_in.at[me_slab],
            obs_send.at[k],
            obs_recv.at[k],
            peer_slab(k),
            me,
        )

    for k in range(1, slabs):
        obs_copy(k).start()

    def store_second(c, at, m, value):
        fields[c, m] = value

    advance(first, store_second)

    def mend_second(mine, theirs, slab, side):
        edge_arrived(mine, slab).wait_recv()
        row = 0 if side == 0 else rows - 1
        for c in range(group):
            at = slice(c * width, (c + 1) * width)
            gain = coefficients(row, side, at)
            for m in range(held):
                fields[c, m, row : row + 1, :] += gain * edge_in[mine, m : m + 1, at]

    edges(1, mend_second)

    def field_copy(k):
        return remote(
            fields.at[peer(k)],
            seen.at[me],
            field_send.at[k],
            field_recv.at[k],
            me_slab,
            peer(k),
        )

    for k in range(1, group):
        field_copy(k).start()
    seen[me] = fields[me]

    for t in range(tiles):
        a, b = iota((span, lanes), 0), iota((span, lanes), 1)
        gather_sel[t * span : (t + 1) * span, :] = (b == t * members + a // rows).astype(
            jnp.bfloat16
        )
    use = jnp.maximum(
        tile_mask[0].astype(jnp.float32),
        (iota((all_tiles, all_tiles), 0) == iota((all_tiles, all_tiles), 1)).astype(jnp.float32),
    ).astype(jnp.bfloat16)
    lane = iota((1, lanes), 1)
    is_gram = lane < packed
    tile_lane = jnp.where(is_gram, lane // members, lane - packed)
    tile_lane = jnp.where(lane < packed + tiles, tile_lane, -1)
    column_lane = jnp.where(is_gram, lax.rem(lane, members), members)
    mine_sel = (
        (iota((all_tiles, lanes), 0) == me * tiles + tile_lane) & (tile_lane >= 0)
    ).astype(jnp.bfloat16)
    use_lane = dot16(use, mine_sel, ((0,), (0,))).astype(jnp.bfloat16)
    sub = iota((lanes, 1), 0)
    sub_gram = sub < packed
    tile_sub = jnp.where(sub_gram, sub // members, sub - packed)
    column_sub = jnp.where(sub_gram, lax.rem(sub, members), members)
    tile_sub = jnp.where(sub < packed + tiles, tile_sub, -all_tiles)
    same_column = (column_lane == column_sub).astype(jnp.float32)
    for d in range(group):
        pick = (iota((lanes, all_tiles), 1) == d * tiles + tile_sub).astype(jnp.bfloat16)
        use_sel[d * lanes : (d + 1) * lanes, :] = (dot16(pick, use_lane) * same_column).astype(
            jnp.bfloat16
        )

    weight, value = obs_out[me_slab, 0], obs_out[me_slab, 1]
    for k in range(1, slabs):
        s = source_slab(k)
        remote(
            obs_in.at[s], obs_in.at[s], obs_send.at[k], obs_recv.at[k], s, me
        ).wait_recv()
        weight = weight + obs_in[s, 0]
        value = value + obs_in[s, 1]

    for k in range(1, group):
        s = source(k)
        remote(
            seen.at[s], seen.at[s], field_send.at[k], field_recv.at[k], me_slab, s
        ).wait_recv()
    total = seen[0, 0]
    for e in range(1, members):
        total = total + seen[e // held, e % held]
    mean = total * (1.0 / members)
    mean_ref[...] = mean
    missing = value - weight * mean
    for e in range(members):
        at = slice(e * rows, (e + 1) * rows)
        dev = seen[e // held, e % held] - mean
        dev_high[at, :], dev_low[at, :] = split2(dev)
        weighted_high[at, :], weighted_low[at, :] = split2(dev * weight)
        innov_rows[e : e + 1, :] = jnp.sum(dev * missing, axis=0, keepdims=True)

    same_row = lax.rem(iota((span, span), 0), rows) == lax.rem(iota((span, span), 1), rows)
    diagonals = []
    for t in range(tiles):
        at = slice(t * PROF, (t + 1) * PROF)
        high = dev_high[:, at]
        gram = dot16(
            jnp.concatenate([weighted_high[:, at], weighted_low[:, at]], axis=1),
            jnp.concatenate([high, high], axis=1),
            ((1,), (1,)),
        ) + dot16(weighted_high[:, at], dev_low[:, at], ((1,), (1,)))
        gram = jnp.where(same_row, gram, 0.0)
        diagonals.append(jnp.sum(gram.reshape(members, rows, span), axis=1))
    packed_part = exact_rows(jnp.concatenate(diagonals, axis=1), gather_sel[...])
    for t in range(tiles):
        innov = jnp.sum(innov_rows[:, t * PROF : (t + 1) * PROF], axis=1, keepdims=True)
        packed_part = packed_part + jnp.where(lane == packed + t, innov, 0.0)
    part[...] = packed_part

    def part_copy(k):
        return remote(
            part, parts.at[me], part_send.at[k], part_recv.at[k], me_slab, peer(k)
        )

    for k in range(1, group):
        part_copy(k).start()
    parts[me] = packed_part
    for k in range(1, group):
        s = source(k)
        remote(
            parts.at[s], parts.at[s], part_send.at[k], part_recv.at[k], me_slab, s
        ).wait_recv()
    sums = exact_rows(jnp.concatenate([parts[d] for d in range(group)], axis=1), use_sel[...])

    a, b = iota((packed, packed), 0), iota((packed, packed), 1)
    same_tile = (a // members) == (b // members)
    identity = (a == b).astype(jnp.float32)
    matrix = jnp.where(
        same_tile, jnp.concatenate([sums[:, :packed]] * tiles, axis=0), 0.0
    ) + (members - 1.0) * identity
    row_sum = jnp.sum(matrix * matrix, axis=1, keepdims=True)
    tile_of = iota((packed, 1), 0) // members
    square = jnp.zeros((packed, 1), jnp.float32)
    for t in range(tiles):
        here = jnp.sum(row_sum[t * members : (t + 1) * members], axis=0, keepdims=True)
        square = jnp.where(tile_of == t, here, square)
    frob = jnp.sqrt(square + 1e-06)
    iterate = matrix / frob
    middle = 1.5 * identity - 0.5 * iterate
    factor = middle
    iterate = dot32(iterate, middle)
    for step in range(1, NS_ITERS):
        middle = 1.5 * identity - 0.5 * dot32(factor, iterate)
        if step < NS_ITERS - 1:
            iterate = dot32(iterate, middle)
        factor = dot32(middle, factor)
    inv_root = factor / jnp.sqrt(frob)
    innov = jnp.concatenate([sums[:, packed + t : packed + t + 1] for t in range(tiles)], axis=0)
    shift = dot32(inv_root, dot32(inv_root, jnp.broadcast_to(innov, (packed, packed))))
    mixing = jnp.where(same_tile, shift + math.sqrt(members - 1.0) * inv_root, 0.0)

    spread_sel = (
        lax.rem(iota((packed, span), 0), members) == iota((packed, span), 1) // rows
    ).astype(jnp.bfloat16)
    mix_high, mix_low = split2(mixing)
    spread_high = dot16(mix_high, spread_sel, ((0,), (0,)))
    spread_low = dot16(mix_low, spread_sel, ((0,), (0,)))
    mean = mean_ref[...]
    for t in range(tiles):
        at = slice(t * PROF, (t + 1) * PROF)

        def grow(spread):
            block = spread[t * members : (t + 1) * members]
            tall = jnp.broadcast_to(block[:, None, :], (members, rows, span)).reshape(span, span)
            return jnp.where(same_row, tall, 0.0).astype(jnp.bfloat16)

        high, low = dev_high[:, at], dev_low[:, at]
        both = dot16(grow(spread_high), jnp.concatenate([high, low], axis=1))
        update = both[:, :PROF] + both[:, PROF:] + dot16(grow(spread_low), high)
        update = update.reshape(members, rows, PROF) + mean[None, :, at]
        for e in range(members):
            result[e // held, e % held, :, at] = update[e]

    columns = pl.ds(pl.multiple_of(me * width, PROF), width)

    def back_copy(k):
        return remote(
            result.at[peer(k)],
            out.at[:, :, columns],
            back_send.at[k],
            back_recv.at[k],
            me_slab,
            peer(k),
        )

    for k in range(1, group):
        back_copy(k).start()
    own = pltpu.make_async_copy(result.at[me], out.at[:, :, columns], own_sem)
    own.start()
    edges(0, lambda mine, theirs, slab, side: edge_copy(mine, theirs, slab).wait_send())
    edges(1, lambda mine, theirs, slab, side: edge_copy(mine, theirs, slab).wait_send())
    for k in range(1, slabs):
        obs_copy(k).wait_send()
    for k in range(1, group):
        field_copy(k).wait_send()
        part_copy(k).wait_send()
    for k in range(1, group):
        s = source(k)
        theirs = pl.ds(pl.multiple_of(s * width, PROF), width)
        back_copy(k).wait_send()
        remote(
            result.at[s], out.at[:, :, theirs], back_send.at[k], back_recv.at[k], me_slab, s
        ).wait_recv()
    own.wait()


def in_one_kernel(
    state, winds, kappa, obs_values, obs_rinv, owner, obs_rows, obs_tiles, counts, tile_mask
):
    slabs, group = lax.axis_size("slab"), lax.axis_size("member")
    held, rows, lon = state.shape
    width = lon // group
    tiles = width // PROF
    members = held * group
    span = members * rows
    packed = tiles * members
    lanes = -(-(packed + tiles) // 128) * 128
    per_slab = owner.shape[0]
    tile_off = obs_tiles - lax.axis_index("member") * tiles
    inside = (
        (tile_off >= 0)
        & (tile_off < tiles)
        & (jnp.arange(per_slab, dtype=jnp.int32) < counts[0])
    )
    target = jnp.where(inside, (owner[:, 0] * tiles + tile_off) * rows + obs_rows, -1)[None, :]
    f32, bf16 = jnp.float32, jnp.bfloat16
    dma = pltpu.SemaphoreType.DMA
    vmem = pl.BlockSpec(memory_space=pltpu.VMEM)
    return pl.pallas_call(
        functools.partial(kernel, slabs, group),
        out_shape=jax.ShapeDtypeStruct(state.shape, f32),
        in_specs=[vmem] * 7,
        out_specs=pl.BlockSpec(memory_space=pl.ANY),
        scratch_shapes=[
            pltpu.VMEM((held, rows, lon), f32),
            pltpu.VMEM((group, held, rows, width), f32),
            pltpu.VMEM((4, held, lon), f32),
            pltpu.VMEM((4, held, lon), f32),
            pltpu.VMEM((slabs, 2, rows, width), f32),
            pltpu.VMEM((slabs, 2, rows, width), f32),
            pltpu.VMEM((group, held, rows, width), f32),
            pltpu.VMEM((members, lanes), f32),
            pltpu.VMEM((group, members, lanes), f32),
            pltpu.VMEM((span, width), bf16),
            pltpu.VMEM((span, width), bf16),
            pltpu.VMEM((span, width), bf16),
            pltpu.VMEM((span, width), bf16),
            pltpu.VMEM((members, width), f32),
            pltpu.VMEM((rows, width), f32),
            pltpu.VMEM((tiles * span, lanes), bf16),
            pltpu.VMEM((group * lanes, lanes), bf16),
            pltpu.VMEM((group, held, rows, width), f32),
            dma((4,)),
            dma((4,)),
            dma((slabs,)),
            dma((slabs,)),
            dma((group,)),
            dma((group,)),
            dma((group,)),
            dma((group,)),
            dma((group,)),
            dma((group,)),
            dma,
        ],
        compiler_params=pltpu.CompilerParams(
            collective_id=0, has_side_effects=True, vmem_limit_bytes=40 * 2**20
        ),
    )(state, winds, kappa, target, obs_values, obs_rinv, tile_mask)


def per_device(state, winds, *rest):
    if state.shape[0] * lax.axis_size("member") * state.shape[1] <= 256:
        return in_one_kernel(state, winds, *rest)
    return on_device(state, winds, *rest)


def solution(mesh):
    placed = (
        P("member", "slab", None),
        P(None, "slab", None),
        P("slab", None),
        P("slab", None),
        P("slab", None),
        P("slab", None),
        P("slab"),
        P("slab"),
        P("slab"),
        P("slab", None, None),
    )
    return jax.shard_map(
        per_device, mesh=mesh, in_specs=placed, out_specs=P("member", "slab", None), check_vma=False
    )
```

```python
import functools
import math

import jax
import jax.numpy as jnp
from jax import lax
from jax.experimental import pallas as pl
from jax.experimental.pallas import tpu as pltpu
from jax.sharding import PartitionSpec as P

PROF = 128
FSTEPS = 2
NS_ITERS = 6


HIGHEST_PRECISION = lax.Precision.HIGHEST


def padded(cells, sides, width):
    for axis, dim in sides:
        count = lax.axis_size(axis)
        ends = count - 1
        head = lax.slice_in_dim(cells, 0, width, axis=dim)
        tail = lax.slice_in_dim(cells, cells.shape[dim] - width, cells.shape[dim], axis=dim)
        cells = jnp.concatenate(
            [
                lax.ppermute(tail, axis, [(i, (i + 1) % count) for i in range(ends)]),
                cells,
                lax.ppermute(head, axis, [((i + 1) % count, i) for i in range(ends)]),
            ],
            axis=dim,
        )
    return cells


def step_forward_border(widened_field, coeff_east, coeff_north, diffusion):
    middle_row = widened_field[:, 1:-1]
    northern_row = widened_field[:, 2:]
    southern_row = widened_field[:, :-2]
    eastern_column = jnp.roll(middle_row, -1, 2)
    western_column = jnp.roll(middle_row, 1, 2)
    return (
        middle_row
        - coeff_east * (eastern_column - western_column) * 0.5
        - coeff_north * (northern_row - southern_row) * 0.5
        + diffusion
        * (eastern_column + western_column + northern_row + southern_row - 4.0 * middle_row)
    )


def inverse_root(matrix, order_size):
    identity = jnp.eye(order_size, dtype=jnp.float32)
    frob_norm = jnp.sqrt(jnp.sum(matrix * matrix, axis=(-2, -1), keepdims=True) + 1e-06)
    iterate = matrix / frob_norm
    factor = jnp.broadcast_to(identity, matrix.shape)
    for step_number in range(NS_ITERS):
        middle = 1.5 * identity - 0.5 * jnp.matmul(factor, iterate, precision=HIGHEST_PRECISION)
        iterate = jnp.matmul(iterate, middle, precision=HIGHEST_PRECISION)
        factor = jnp.matmul(middle, factor, precision=HIGHEST_PRECISION)
    return factor / jnp.sqrt(frob_norm)


def weights_for(gram_total, innov_total, members):
    identity = jnp.eye(members, dtype=jnp.float32)
    inv_root = inverse_root(gram_total + (members - 1.0) * identity, members)
    half_step = jnp.einsum("...ij,...j->...i", inv_root, innov_total, precision=HIGHEST_PRECISION)
    mean_shift = jnp.einsum("...ij,...j->...i", inv_root, half_step, precision=HIGHEST_PRECISION)
    return mean_shift[..., :, None] + math.sqrt(members - 1.0) * inv_root


def on_device(
    state, winds, kappa, obs_values, obs_rinv, owner, obs_rows, obs_tiles, counts, tile_mask
):
    lat_rows = state.shape[1]
    predict_members = state
    for step_number in range(FSTEPS):
        widened_field = padded(predict_members, (("slab", 1),), 1)
        predict_members = step_forward_border(widened_field, winds[0], winds[1], kappa)
    cell_major_layout = lax.all_to_all(
        predict_members, "member", split_axis=2, concat_axis=0, tiled=True
    )
    ensemble = cell_major_layout.shape[0]
    cell_width = cell_major_layout.shape[2]
    tiles_here = cell_width // PROF
    ensemble_average = jnp.mean(cell_major_layout, axis=0)
    member_deviation = cell_major_layout - ensemble_average
    slab_count = lax.axis_size("slab")
    per_slab = owner.shape[0]
    first_tile = lax.axis_index("member") * tiles_here
    cells = lat_rows * tiles_here
    tile_off = obs_tiles - first_tile
    inside = (
        (tile_off >= 0)
        & (tile_off < tiles_here)
        & (jnp.arange(per_slab, dtype=jnp.int32) < counts[0])
    )
    target = jnp.where(
        inside, owner[:, 0] * cells + obs_rows * tiles_here + tile_off, -1
    )
    placing = (
        target[None, :] == jnp.arange(slab_count * cells, dtype=jnp.int32)[:, None]
    ).astype(jnp.float32)
    payload = jnp.concatenate([obs_rinv, obs_rinv * obs_values], axis=1)
    sums = jnp.matmul(placing, payload, precision=HIGHEST_PRECISION)
    sums = lax.all_to_all(
        sums.reshape(slab_count, lat_rows, tiles_here, 2, PROF),
        "slab",
        split_axis=0,
        concat_axis=0,
        tiled=True,
    )
    sums = jnp.sum(sums, axis=0)
    cell_weight, cell_value = sums[:, :, 0], sums[:, :, 1]
    blocks = member_deviation.reshape(ensemble, lat_rows, tiles_here, PROF)
    mean_blocks = ensemble_average.reshape(lat_rows, tiles_here, PROF)
    gram_here = jnp.einsum(
        "irth,jrth->tij", blocks * cell_weight, blocks, precision=HIGHEST_PRECISION
    )
    innov_here = jnp.einsum(
        "irth,rth->ti",
        blocks,
        cell_value - cell_weight * mean_blocks,
        precision=HIGHEST_PRECISION,
    )
    tile_count = tile_mask.shape[1]
    tile_use = jnp.maximum(tile_mask[0].astype(jnp.float32), jnp.eye(tile_count, dtype=jnp.float32))
    use_mine = lax.dynamic_slice_in_dim(tile_use, first_tile, tiles_here, 0)
    gram_next = jnp.einsum(
        "ts,sij->tij",
        use_mine,
        lax.all_gather(gram_here, "member", axis=0, tiled=True),
        precision=HIGHEST_PRECISION,
    )
    innov_next = jnp.einsum(
        "ts,si->ti",
        use_mine,
        lax.all_gather(innov_here, "member", axis=0, tiled=True),
        precision=HIGHEST_PRECISION,
    )
    mixing = weights_for(gram_next, innov_next, ensemble)
    update = jnp.einsum("irth,tij->jrth", blocks, mixing, precision=HIGHEST_PRECISION)
    update = update + ensemble_average.reshape(lat_rows, tiles_here, PROF)
    return lax.all_to_all(
        update.reshape(ensemble, lat_rows, cell_width),
        "member",
        split_axis=0,
        concat_axis=2,
        tiled=True,
    )


def split3(x):
    high = x.astype(jnp.bfloat16)
    rest = x - high.astype(jnp.float32)
    middle = rest.astype(jnp.bfloat16)
    low = (rest - middle.astype(jnp.float32)).astype(jnp.bfloat16)
    return high, middle, low


def split2(x):
    high = x.astype(jnp.bfloat16)
    return high, (x - high.astype(jnp.float32)).astype(jnp.bfloat16)


def dot16(a, b, dims=((1,), (0,))):
    return lax.dot_general(a, b, (dims, ((), ())), preferred_element_type=jnp.float32)


def dot32(a, b, dims=((1,), (0,))):
    return lax.dot_general(
        a,
        b,
        (dims, ((), ())),
        precision=HIGHEST_PRECISION,
        preferred_element_type=jnp.float32,
    )


def iota(shape, dim):
    return lax.broadcasted_iota(jnp.int32, shape, dim)


def exact_rows(x, ones):
    rows = x.shape[0]
    whole = dot16(jnp.concatenate(split3(x), axis=0), ones)
    return whole[:rows] + whole[rows : 2 * rows] + whole[2 * rows :]


def kernel(
    slabs,
    group,
    state_hbm,
    winds_hbm,
    kappa_hbm,
    values_hbm,
    rinv_hbm,
    owner_hbm,
    rows_hbm,
    tiles_hbm,
    counts,
    mask_hbm,
    out,
    state,
    winds,
    kappa,
    obs_values,
    obs_rinv,
    owner,
    obs_rows,
    obs_tiles,
    tile_mask,
    load_sem,
    first,
    fields,
    edge_out,
    edge_in,
    obs_out,
    obs_in,
    seen,
    ordered,
    part,
    parts,
    dev_high,
    dev_low,
    weighted_high,
    weighted_low,
    innov_rows,
    mean_ref,
    gather_sel,
    use_sel,
    result,
    edge_send,
    edge_recv,
    obs_send,
    obs_recv,
    field_send,
    field_recv,
    part_send,
    part_recv,
    back_send,
    back_recv,
    own_sem,
):
    me_slab, me = lax.axis_index("slab"), lax.axis_index("member")
    held, rows, lon = state.shape
    width = lon // group
    tiles = width // PROF
    members = held * group
    span = members * rows
    lanes = part.shape[1]
    packed = tiles * members
    all_tiles = tile_mask.shape[1]

    def peer(k):
        return lax.rem(me + k, group)

    def source(k):
        return lax.rem(me + group - k, group)

    def peer_slab(k):
        return lax.rem(me_slab + k, slabs)

    def source_slab(k):
        return lax.rem(me_slab + slabs - k, slabs)

    def remote(src, dst, send, recv, slab, member):
        return pltpu.make_async_remote_copy(
            src_ref=src,
            dst_ref=dst,
            send_sem=send,
            recv_sem=recv,
            device_id=(slab, member),
            device_id_type=pl.DeviceIdType.MESH,
        )

    loads = [
        pltpu.make_async_copy(src, dst, load_sem.at[n])
        for n, (src, dst) in enumerate(
            (
                (owner_hbm, owner),
                (rows_hbm, obs_rows),
                (tiles_hbm, obs_tiles),
                (rinv_hbm, obs_rinv),
                (values_hbm, obs_values),
                (state_hbm, state),
                (winds_hbm, winds),
                (kappa_hbm, kappa),
                (mask_hbm, tile_mask),
            )
        )
    ]
    for load in loads:
        load.start()

    barrier = pltpu.get_barrier_semaphore()
    for k in range(1, group):
        pl.semaphore_signal(
            barrier, inc=1, device_id=(me_slab, peer(k)), device_id_type=pl.DeviceIdType.MESH
        )
    for k in range(1, slabs):
        pl.semaphore_signal(
            barrier, inc=1, device_id=(peer_slab(k), me), device_id_type=pl.DeviceIdType.MESH
        )

    cells = slabs * tiles * rows
    for load in loads[:5]:
        load.wait()
    per_slab = owner.shape[1]
    tile_off = obs_tiles[...] - me * tiles
    inside = (tile_off >= 0) & (tile_off < tiles) & (iota((1, per_slab), 1) < counts[0])
    target = jnp.where(inside, (owner[...] * tiles + tile_off) * rows + obs_rows[...], -1)
    placing = (iota((cells, per_slab), 0) == target).astype(jnp.bfloat16)
    rinv = obs_rinv[...]
    payload = jnp.concatenate([rinv, rinv * obs_values[...]], axis=1)
    sums = sum(dot16(placing, piece) for piece in split3(payload))
    for o in range(slabs):
        for t in range(tiles):
            at = (o * tiles + t) * rows
            obs_out[o, 0, :, t * PROF : (t + 1) * PROF] = sums[at : at + rows, :PROF]
            obs_out[o, 1, :, t * PROF : (t + 1) * PROF] = sums[at : at + rows, PROF:]
    loads[5].wait()
    for m in range(held):
        edge_out[0, m : m + 1, :] = state[m, 0:1, :]
        edge_out[1, m : m + 1, :] = state[m, rows - 1 : rows, :]

    for load in loads[6:]:
        load.wait()

    pl.semaphore_wait(barrier, group + slabs - 2)

    def edges(step, act):
        south, north = 2 * step, 2 * step + 1

        @pl.when(me_slab > 0)
        def _():
            act(south, north, me_slab - 1, 0)

        @pl.when(me_slab < slabs - 1)
        def _():
            act(north, south, me_slab + 1, 1)

    def edge_copy(mine, theirs, slab):
        return remote(
            edge_out.at[mine],
            edge_in.at[theirs],
            edge_send.at[mine],
            edge_recv.at[theirs],
            slab,
            me,
        )

    def edge_arrived(mine, slab):
        return remote(
            edge_out.at[mine],
            edge_in.at[mine],
            edge_send.at[mine],
            edge_recv.at[mine],
            slab,
            me,
        )

    def coefficients(row, side, at):
        sign = 0.5 if side == 0 else -0.5
        return sign * winds[1, row : row + 1, at] + kappa[row : row + 1, at]

    def advance(load, store):
        def body(c, carry):
            advance_at(load, store, c)
            return carry

        lax.fori_loop(0, group, body, 0)

    def advance_at(load, store, c):
        at = pl.multiple_of(c * width, PROF)
        before = pl.multiple_of(lax.rem(c * width + lon - PROF, lon), PROF)
        after = pl.multiple_of(lax.rem(c * width + width, lon), PROF)
        east_wind = 0.5 * winds[0, :, pl.ds(at, width)]
        north_wind = 0.5 * winds[1, :, pl.ds(at, width)]
        mix = kappa[:, pl.ds(at, width)]
        row = iota((rows, width), 0)
        for m in range(held):
            cell = load[m, :, pl.ds(at, width)]
            wide = jnp.concatenate(
                [load[m, :, pl.ds(before, PROF)], cell, load[m, :, pl.ds(after, PROF)]], axis=1
            )
            east = pltpu.roll(wide, width + 2 * PROF - 1, 1)[:, PROF : PROF + width]
            west = pltpu.roll(wide, 1, 1)[:, PROF : PROF + width]
            north = jnp.where(row == rows - 1, 0.0, pltpu.roll(cell, rows - 1, 0))
            south = jnp.where(row == 0, 0.0, pltpu.roll(cell, 1, 0))
            store(
                c,
                at,
                m,
                cell
                - east_wind * (east - west)
                - north_wind * (north - south)
                + mix * (east + west + north + south - 4.0 * cell),
            )

    edges(0, lambda mine, theirs, slab, side: edge_copy(mine, theirs, slab).start())

    def store_first(c, at, m, value):
        first[m, :, pl.ds(at, width)] = value

    advance(state, store_first)

    inner = rows - 4
    bulk = held * inner

    def store_inner(c, at, m, value):
        fields[c, m * inner : (m + 1) * inner, :] = value[2 : rows - 2]

    def inner_copy(k):
        return remote(
            fields.at[peer(k), 0:bulk],
            seen.at[me, 0:bulk],
            field_send.at[k],
            field_recv.at[k],
            me_slab,
            peer(k),
        )

    def send_inner(k, carry):
        advance_at(first, store_inner, peer(k))
        inner_copy(k).start()
        return carry

    lax.fori_loop(1, group, send_inner, 0)
    advance_at(first, store_inner, me)

    def mend_first(mine, theirs, slab, side):
        edge_arrived(mine, slab).wait_recv()
        row = 0 if side == 0 else rows - 1
        gain = coefficients(row, side, slice(None))
        for m in range(held):
            first[m, row : row + 1, :] += gain * edge_in[mine, m : m + 1, :]

    edges(0, mend_first)
    for m in range(held):
        edge_out[2, m : m + 1, :] = first[m, 0:1, :]
        edge_out[3, m : m + 1, :] = first[m, rows - 1 : rows, :]
    edges(1, lambda mine, theirs, slab, side: edge_copy(mine, theirs, slab).start())

    def obs_copy(k):
        return remote(
            obs_out.at[peer_slab(k)],
            obs_in.at[me_slab],
            obs_send.at[k],
            obs_recv.at[k],
            peer_slab(k),
            me,
        )

    for k in range(1, slabs):
        obs_copy(k).start()

    def store_rim(c, at, m, value):
        row = bulk + 4 * m
        fields[c, row : row + 2, :] = value[0:2]
        fields[c, row + 2 : row + 4, :] = value[rows - 2 : rows]

    advance(first, store_rim)

    def mend_second(mine, theirs, slab, side):
        edge_arrived(mine, slab).wait_recv()
        row = 0 if side == 0 else rows - 1
        for c in range(group):
            at = slice(c * width, (c + 1) * width)
            gain = coefficients(row, side, at)
            for m in range(held):
                place = bulk + 4 * m + 3 * side
                fields[c, place : place + 1, :] += gain * edge_in[mine, m : m + 1, at]

    edges(1, mend_second)

    def rim_copy(k):
        return remote(
            fields.at[peer(k), bulk : held * rows],
            seen.at[me, bulk : held * rows],
            field_send.at[group + k],
            field_recv.at[group + k],
            me_slab,
            peer(k),
        )

    for k in range(1, group):
        rim_copy(k).start()
    seen[me] = fields[me]

    for t in range(tiles):
        a, b = iota((span, lanes), 0), iota((span, lanes), 1)
        gather_sel[t * span : (t + 1) * span, :] = (b == t * members + a // rows).astype(
            jnp.bfloat16
        )
    use = jnp.maximum(
        tile_mask[0].astype(jnp.float32),
        (iota((all_tiles, all_tiles), 0) == iota((all_tiles, all_tiles), 1)).astype(jnp.float32),
    ).astype(jnp.bfloat16)
    lane = iota((1, lanes), 1)
    is_gram = lane < packed
    tile_lane = jnp.where(is_gram, lane // members, lane - packed)
    tile_lane = jnp.where(lane < packed + tiles, tile_lane, -1)
    column_lane = jnp.where(is_gram, lax.rem(lane, members), members)
    mine_sel = (
        (iota((all_tiles, lanes), 0) == me * tiles + tile_lane) & (tile_lane >= 0)
    ).astype(jnp.bfloat16)
    use_lane = dot16(use, mine_sel, ((0,), (0,))).astype(jnp.bfloat16)
    sub = iota((lanes, 1), 0)
    sub_gram = sub < packed
    tile_sub = jnp.where(sub_gram, sub // members, sub - packed)
    column_sub = jnp.where(sub_gram, lax.rem(sub, members), members)
    tile_sub = jnp.where(sub < packed + tiles, tile_sub, -all_tiles)
    same_column = (column_lane == column_sub).astype(jnp.float32)
    for d in range(group):
        pick = (iota((lanes, all_tiles), 1) == d * tiles + tile_sub).astype(jnp.bfloat16)
        use_sel[d * lanes : (d + 1) * lanes, :] = (dot16(pick, use_lane) * same_column).astype(
            jnp.bfloat16
        )

    weight, value = obs_out[me_slab, 0], obs_out[me_slab, 1]
    for k in range(1, slabs):
        s = source_slab(k)
        remote(
            obs_in.at[s], obs_in.at[s], obs_send.at[k], obs_recv.at[k], s, me
        ).wait_recv()
        weight = weight + obs_in[s, 0]
        value = value + obs_in[s, 1]

    for k in range(1, group):
        s = source(k)
        for n, at in ((k, slice(0, bulk)), (group + k, slice(bulk, held * rows))):
            remote(
                seen.at[s, at], seen.at[s, at], field_send.at[n], field_recv.at[n], me_slab, s
            ).wait_recv()

    def field(e):
        d, m = e // held, e % held
        rim = bulk + 4 * m
        return jnp.concatenate(
            [
                seen[d, rim : rim + 2, :],
                seen[d, m * inner : (m + 1) * inner, :],
                seen[d, rim + 2 : rim + 4, :],
            ],
            axis=0,
        )

    total = jnp.zeros((rows, width), jnp.float32)
    for e in range(members):
        cell = field(e)
        ordered[e] = cell
        total = total + cell
    mean = total * (1.0 / members)
    mean_ref[...] = mean
    missing = value - weight * mean
    for e in range(members):
        at = slice(e * rows, (e + 1) * rows)
        dev = ordered[e] - mean
        dev_high[at, :], dev_low[at, :] = split2(dev)
        weighted_high[at, :], weighted_low[at, :] = split2(dev * weight)
        innov_rows[e : e + 1, :] = jnp.sum(dev * missing, axis=0, keepdims=True)

    same_row = lax.rem(iota((span, span), 0), rows) == lax.rem(iota((span, span), 1), rows)
    diagonals = []
    for t in range(tiles):
        at = slice(t * PROF, (t + 1) * PROF)
        high = dev_high[:, at]
        gram = dot16(
            jnp.concatenate([weighted_high[:, at], weighted_low[:, at]], axis=1),
            jnp.concatenate([high, high], axis=1),
            ((1,), (1,)),
        ) + dot16(weighted_high[:, at], dev_low[:, at], ((1,), (1,)))
        gram = jnp.where(same_row, gram, 0.0)
        diagonals.append(jnp.sum(gram.reshape(members, rows, span), axis=1))
    packed_part = exact_rows(jnp.concatenate(diagonals, axis=1), gather_sel[...])
    for t in range(tiles):
        innov = jnp.sum(innov_rows[:, t * PROF : (t + 1) * PROF], axis=1, keepdims=True)
        packed_part = packed_part + jnp.where(lane == packed + t, innov, 0.0)
    part[...] = packed_part

    def part_copy(k):
        return remote(
            part, parts.at[me], part_send.at[k], part_recv.at[k], me_slab, peer(k)
        )

    for k in range(1, group):
        part_copy(k).start()
    parts[me] = packed_part
    for k in range(1, group):
        s = source(k)
        remote(
            parts.at[s], parts.at[s], part_send.at[k], part_recv.at[k], me_slab, s
        ).wait_recv()
    sums = exact_rows(jnp.concatenate([parts[d] for d in range(group)], axis=1), use_sel[...])

    a, b = iota((packed, packed), 0), iota((packed, packed), 1)
    same_tile = (a // members) == (b // members)
    identity = (a == b).astype(jnp.float32)
    matrix = jnp.where(
        same_tile, jnp.concatenate([sums[:, :packed]] * tiles, axis=0), 0.0
    ) + (members - 1.0) * identity
    row_sum = jnp.sum(matrix * matrix, axis=1, keepdims=True)
    tile_of = iota((packed, 1), 0) // members
    square = jnp.zeros((packed, 1), jnp.float32)
    for t in range(tiles):
        here = jnp.sum(row_sum[t * members : (t + 1) * members], axis=0, keepdims=True)
        square = jnp.where(tile_of == t, here, square)
    frob = jnp.sqrt(square + 1e-06)
    iterate = matrix / frob
    middle = 1.5 * identity - 0.5 * iterate
    factor = middle
    iterate = dot32(iterate, middle)
    for step in range(1, NS_ITERS):
        middle = 1.5 * identity - 0.5 * dot32(factor, iterate)
        if step < NS_ITERS - 1:
            iterate = dot32(iterate, middle)
        factor = dot32(middle, factor)
    inv_root = factor / jnp.sqrt(frob)
    innov = jnp.concatenate([sums[:, packed + t : packed + t + 1] for t in range(tiles)], axis=0)
    shift = dot32(inv_root, dot32(inv_root, jnp.broadcast_to(innov, (packed, packed))))
    mixing = jnp.where(same_tile, shift + math.sqrt(members - 1.0) * inv_root, 0.0)

    spread_sel = (
        lax.rem(iota((packed, span), 0), members) == iota((packed, span), 1) // rows
    ).astype(jnp.bfloat16)
    mix_high, mix_low = split2(mixing)
    spread_high = dot16(mix_high, spread_sel, ((0,), (0,)))
    spread_low = dot16(mix_low, spread_sel, ((0,), (0,)))
    mean = mean_ref[...]
    for t in range(tiles):
        at = slice(t * PROF, (t + 1) * PROF)

        def grow(spread):
            block = spread[t * members : (t + 1) * members]
            tall = jnp.broadcast_to(block[:, None, :], (members, rows, span)).reshape(span, span)
            return jnp.where(same_row, tall, 0.0).astype(jnp.bfloat16)

        high, low = dev_high[:, at], dev_low[:, at]
        both = dot16(grow(spread_high), jnp.concatenate([high, low], axis=1))
        update = both[:, :PROF] + both[:, PROF:] + dot16(grow(spread_low), high)
        update = update.reshape(members, rows, PROF) + mean[None, :, at]
        for e in range(members):
            result[e // held, e % held, :, at] = update[e]

    columns = pl.ds(pl.multiple_of(me * width, PROF), width)

    def back_copy(k):
        return remote(
            result.at[peer(k)],
            out.at[:, :, columns],
            back_send.at[k],
            back_recv.at[k],
            me_slab,
            peer(k),
        )

    for k in range(1, group):
        back_copy(k).start()
    own = pltpu.make_async_copy(result.at[me], out.at[:, :, columns], own_sem)
    own.start()
    edges(0, lambda mine, theirs, slab, side: edge_copy(mine, theirs, slab).wait_send())
    edges(1, lambda mine, theirs, slab, side: edge_copy(mine, theirs, slab).wait_send())
    for k in range(1, slabs):
        obs_copy(k).wait_send()
    for k in range(1, group):
        inner_copy(k).wait_send()
        rim_copy(k).wait_send()
        part_copy(k).wait_send()
    for k in range(1, group):
        s = source(k)
        theirs = pl.ds(pl.multiple_of(s * width, PROF), width)
        back_copy(k).wait_send()
        remote(
            result.at[s], out.at[:, :, theirs], back_send.at[k], back_recv.at[k], me_slab, s
        ).wait_recv()
    own.wait()


def in_one_kernel(
    state, winds, kappa, obs_values, obs_rinv, owner, obs_rows, obs_tiles, counts, tile_mask
):
    slabs, group = lax.axis_size("slab"), lax.axis_size("member")
    held, rows, lon = state.shape
    width = lon // group
    tiles = width // PROF
    members = held * group
    span = members * rows
    packed = tiles * members
    lanes = -(-(packed + tiles) // 128) * 128
    f32, bf16 = jnp.float32, jnp.bfloat16
    dma = pltpu.SemaphoreType.DMA
    hbm = pl.BlockSpec(memory_space=pltpu.HBM)
    return pl.pallas_call(
        functools.partial(kernel, slabs, group),
        out_shape=jax.ShapeDtypeStruct(state.shape, f32),
        in_specs=[hbm] * 8 + [pl.BlockSpec(memory_space=pltpu.SMEM), hbm],
        out_specs=pl.BlockSpec(memory_space=pl.ANY),
        scratch_shapes=[
            pltpu.VMEM(state.shape, f32),
            pltpu.VMEM(winds.shape, f32),
            pltpu.VMEM(kappa.shape, f32),
            pltpu.VMEM(obs_values.shape, f32),
            pltpu.VMEM(obs_rinv.shape, f32),
            pltpu.VMEM((1, owner.shape[0]), jnp.int32),
            pltpu.VMEM((1, owner.shape[0]), jnp.int32),
            pltpu.VMEM((1, owner.shape[0]), jnp.int32),
            pltpu.VMEM(tile_mask.shape, jnp.int32),
            dma((9,)),
            pltpu.VMEM((held, rows, lon), f32),
            pltpu.VMEM((group, held * rows, width), f32),
            pltpu.VMEM((4, held, lon), f32),
            pltpu.VMEM((4, held, lon), f32),
            pltpu.VMEM((slabs, 2, rows, width), f32),
            pltpu.VMEM((slabs, 2, rows, width), f32),
            pltpu.VMEM((group, held * rows, width), f32),
            pltpu.VMEM((members, rows, width), f32),
            pltpu.VMEM((members, lanes), f32),
            pltpu.VMEM((group, members, lanes), f32),
            pltpu.VMEM((span, width), bf16),
            pltpu.VMEM((span, width), bf16),
            pltpu.VMEM((span, width), bf16),
            pltpu.VMEM((span, width), bf16),
            pltpu.VMEM((members, width), f32),
            pltpu.VMEM((rows, width), f32),
            pltpu.VMEM((tiles * span, lanes), bf16),
            pltpu.VMEM((group * lanes, lanes), bf16),
            pltpu.VMEM((group, held, rows, width), f32),
            dma((4,)),
            dma((4,)),
            dma((slabs,)),
            dma((slabs,)),
            dma((2 * group,)),
            dma((2 * group,)),
            dma((group,)),
            dma((group,)),
            dma((group,)),
            dma((group,)),
            dma,
        ],
        compiler_params=pltpu.CompilerParams(
            collective_id=0, has_side_effects=True, vmem_limit_bytes=62 * 2**20
        ),
    )(
        state,
        winds,
        kappa,
        obs_values,
        obs_rinv,
        owner[:, 0][None, :],
        obs_rows[None, :],
        obs_tiles[None, :],
        counts,
        tile_mask,
    )


def per_device(state, winds, *rest):
    held, rows = state.shape[:2]
    spare = held * (rows - 4) % 8
    if held * lax.axis_size("member") * rows <= 256 and spare == 0:
        return in_one_kernel(state, winds, *rest)
    return on_device(state, winds, *rest)


def solution(mesh):
    placed = (
        P("member", "slab", None),
        P(None, "slab", None),
        P("slab", None),
        P("slab", None),
        P("slab", None),
        P("slab", None),
        P("slab"),
        P("slab"),
        P("slab"),
        P("slab", None, None),
    )
    return jax.shard_map(
        per_device, mesh=mesh, in_specs=placed, out_specs=P("member", "slab", None), check_vma=False
    )
```

```python
import functools
import math

import jax
import jax.numpy as jnp
from jax import lax
from jax.experimental import pallas as pl
from jax.experimental.pallas import tpu as pltpu
from jax.sharding import PartitionSpec as P

PROF = 128
FSTEPS = 2
NS_ITERS = 6


HIGHEST_PRECISION = lax.Precision.HIGHEST


def padded(cells, sides, width):
    for axis, dim in sides:
        count = lax.axis_size(axis)
        ends = count - 1
        head = lax.slice_in_dim(cells, 0, width, axis=dim)
        tail = lax.slice_in_dim(cells, cells.shape[dim] - width, cells.shape[dim], axis=dim)
        cells = jnp.concatenate(
            [
                lax.ppermute(tail, axis, [(i, (i + 1) % count) for i in range(ends)]),
                cells,
                lax.ppermute(head, axis, [((i + 1) % count, i) for i in range(ends)]),
            ],
            axis=dim,
        )
    return cells


def step_forward_border(widened_field, coeff_east, coeff_north, diffusion):
    middle_row = widened_field[:, 1:-1]
    northern_row = widened_field[:, 2:]
    southern_row = widened_field[:, :-2]
    eastern_column = jnp.roll(middle_row, -1, 2)
    western_column = jnp.roll(middle_row, 1, 2)
    return (
        middle_row
        - coeff_east * (eastern_column - western_column) * 0.5
        - coeff_north * (northern_row - southern_row) * 0.5
        + diffusion
        * (eastern_column + western_column + northern_row + southern_row - 4.0 * middle_row)
    )


def inverse_root(matrix, order_size):
    identity = jnp.eye(order_size, dtype=jnp.float32)
    frob_norm = jnp.sqrt(jnp.sum(matrix * matrix, axis=(-2, -1), keepdims=True) + 1e-06)
    iterate = matrix / frob_norm
    factor = jnp.broadcast_to(identity, matrix.shape)
    for step_number in range(NS_ITERS):
        middle = 1.5 * identity - 0.5 * jnp.matmul(factor, iterate, precision=HIGHEST_PRECISION)
        iterate = jnp.matmul(iterate, middle, precision=HIGHEST_PRECISION)
        factor = jnp.matmul(middle, factor, precision=HIGHEST_PRECISION)
    return factor / jnp.sqrt(frob_norm)


def weights_for(gram_total, innov_total, members):
    identity = jnp.eye(members, dtype=jnp.float32)
    inv_root = inverse_root(gram_total + (members - 1.0) * identity, members)
    half_step = jnp.einsum("...ij,...j->...i", inv_root, innov_total, precision=HIGHEST_PRECISION)
    mean_shift = jnp.einsum("...ij,...j->...i", inv_root, half_step, precision=HIGHEST_PRECISION)
    return mean_shift[..., :, None] + math.sqrt(members - 1.0) * inv_root


def on_device(
    state, winds, kappa, obs_values, obs_rinv, owner, obs_rows, obs_tiles, counts, tile_mask
):
    lat_rows = state.shape[1]
    predict_members = state
    for step_number in range(FSTEPS):
        widened_field = padded(predict_members, (("slab", 1),), 1)
        predict_members = step_forward_border(widened_field, winds[0], winds[1], kappa)
    cell_major_layout = lax.all_to_all(
        predict_members, "member", split_axis=2, concat_axis=0, tiled=True
    )
    ensemble = cell_major_layout.shape[0]
    cell_width = cell_major_layout.shape[2]
    tiles_here = cell_width // PROF
    ensemble_average = jnp.mean(cell_major_layout, axis=0)
    member_deviation = cell_major_layout - ensemble_average
    slab_count = lax.axis_size("slab")
    per_slab = owner.shape[0]
    first_tile = lax.axis_index("member") * tiles_here
    cells = lat_rows * tiles_here
    tile_off = obs_tiles - first_tile
    inside = (
        (tile_off >= 0)
        & (tile_off < tiles_here)
        & (jnp.arange(per_slab, dtype=jnp.int32) < counts[0])
    )
    target = jnp.where(
        inside, owner[:, 0] * cells + obs_rows * tiles_here + tile_off, -1
    )
    placing = (
        target[None, :] == jnp.arange(slab_count * cells, dtype=jnp.int32)[:, None]
    ).astype(jnp.float32)
    payload = jnp.concatenate([obs_rinv, obs_rinv * obs_values], axis=1)
    sums = jnp.matmul(placing, payload, precision=HIGHEST_PRECISION)
    sums = lax.all_to_all(
        sums.reshape(slab_count, lat_rows, tiles_here, 2, PROF),
        "slab",
        split_axis=0,
        concat_axis=0,
        tiled=True,
    )
    sums = jnp.sum(sums, axis=0)
    cell_weight, cell_value = sums[:, :, 0], sums[:, :, 1]
    blocks = member_deviation.reshape(ensemble, lat_rows, tiles_here, PROF)
    mean_blocks = ensemble_average.reshape(lat_rows, tiles_here, PROF)
    gram_here = jnp.einsum(
        "irth,jrth->tij", blocks * cell_weight, blocks, precision=HIGHEST_PRECISION
    )
    innov_here = jnp.einsum(
        "irth,rth->ti",
        blocks,
        cell_value - cell_weight * mean_blocks,
        precision=HIGHEST_PRECISION,
    )
    tile_count = tile_mask.shape[1]
    tile_use = jnp.maximum(tile_mask[0].astype(jnp.float32), jnp.eye(tile_count, dtype=jnp.float32))
    use_mine = lax.dynamic_slice_in_dim(tile_use, first_tile, tiles_here, 0)
    gram_next = jnp.einsum(
        "ts,sij->tij",
        use_mine,
        lax.all_gather(gram_here, "member", axis=0, tiled=True),
        precision=HIGHEST_PRECISION,
    )
    innov_next = jnp.einsum(
        "ts,si->ti",
        use_mine,
        lax.all_gather(innov_here, "member", axis=0, tiled=True),
        precision=HIGHEST_PRECISION,
    )
    mixing = weights_for(gram_next, innov_next, ensemble)
    update = jnp.einsum("irth,tij->jrth", blocks, mixing, precision=HIGHEST_PRECISION)
    update = update + ensemble_average.reshape(lat_rows, tiles_here, PROF)
    return lax.all_to_all(
        update.reshape(ensemble, lat_rows, cell_width),
        "member",
        split_axis=0,
        concat_axis=2,
        tiled=True,
    )


def split3(x):
    high = x.astype(jnp.bfloat16)
    rest = x - high.astype(jnp.float32)
    middle = rest.astype(jnp.bfloat16)
    low = (rest - middle.astype(jnp.float32)).astype(jnp.bfloat16)
    return high, middle, low


def split2(x):
    high = x.astype(jnp.bfloat16)
    return high, (x - high.astype(jnp.float32)).astype(jnp.bfloat16)


def dot16(a, b, dims=((1,), (0,))):
    return lax.dot_general(a, b, (dims, ((), ())), preferred_element_type=jnp.float32)


def dot32(a, b, dims=((1,), (0,))):
    return lax.dot_general(
        a,
        b,
        (dims, ((), ())),
        precision=HIGHEST_PRECISION,
        preferred_element_type=jnp.float32,
    )


def iota(shape, dim):
    return lax.broadcasted_iota(jnp.int32, shape, dim)


def exact_rows(x, ones):
    rows = x.shape[0]
    whole = dot16(jnp.concatenate(split3(x), axis=0), ones)
    return whole[:rows] + whole[rows : 2 * rows] + whole[2 * rows :]


def kernel(
    slabs,
    group,
    state_hbm,
    winds_hbm,
    kappa_hbm,
    values_hbm,
    rinv_hbm,
    owner_hbm,
    rows_hbm,
    tiles_hbm,
    counts,
    mask_hbm,
    out,
    state,
    winds,
    kappa,
    obs_values,
    obs_rinv,
    owner,
    obs_rows,
    obs_tiles,
    tile_mask,
    load_sem,
    first,
    fields,
    edge_out,
    edge_in,
    obs_out,
    obs_in,
    seen,
    ordered,
    part,
    parts,
    dev_high,
    dev_low,
    weighted_high,
    weighted_low,
    innov_rows,
    mean_ref,
    gather_sel,
    use_sel,
    result,
    edge_send,
    edge_recv,
    obs_send,
    obs_recv,
    field_send,
    field_recv,
    part_send,
    part_recv,
    back_send,
    back_recv,
    own_sem,
):
    me_slab, me = lax.axis_index("slab"), lax.axis_index("member")
    held, rows, lon = state.shape
    width = lon // group
    tiles = width // PROF
    members = held * group
    span = members * rows
    lanes = part.shape[1]
    packed = tiles * members
    all_tiles = tile_mask.shape[1]

    def peer(k):
        return lax.rem(me + k, group)

    def source(k):
        return lax.rem(me + group - k, group)

    def peer_slab(k):
        return lax.rem(me_slab + k, slabs)

    def source_slab(k):
        return lax.rem(me_slab + slabs - k, slabs)

    def remote(src, dst, send, recv, slab, member):
        return pltpu.make_async_remote_copy(
            src_ref=src,
            dst_ref=dst,
            send_sem=send,
            recv_sem=recv,
            device_id=(slab, member),
            device_id_type=pl.DeviceIdType.MESH,
        )

    barrier = pltpu.get_barrier_semaphore()
    for k in range(1, group):
        pl.semaphore_signal(
            barrier, inc=1, device_id=(me_slab, peer(k)), device_id_type=pl.DeviceIdType.MESH
        )
    for k in range(1, slabs):
        pl.semaphore_signal(
            barrier, inc=1, device_id=(peer_slab(k), me), device_id_type=pl.DeviceIdType.MESH
        )

    loads = [
        pltpu.make_async_copy(src, dst, load_sem.at[n])
        for n, (src, dst) in enumerate(
            (
                (owner_hbm, owner),
                (rows_hbm, obs_rows),
                (tiles_hbm, obs_tiles),
                (rinv_hbm, obs_rinv),
                (values_hbm, obs_values),
                (state_hbm, state),
                (winds_hbm, winds),
                (kappa_hbm, kappa),
                (mask_hbm, tile_mask),
            )
        )
    ]
    for load in loads:
        load.start()

    cells = slabs * tiles * rows
    for load in loads[:5]:
        load.wait()
    per_slab = owner.shape[1]
    tile_off = obs_tiles[...] - me * tiles
    inside = (tile_off >= 0) & (tile_off < tiles) & (iota((1, per_slab), 1) < counts[0])
    target = jnp.where(inside, (owner[...] * tiles + tile_off) * rows + obs_rows[...], -1)
    placing = (iota((cells, per_slab), 0) == target).astype(jnp.bfloat16)
    rinv = obs_rinv[...]
    payload = jnp.concatenate([rinv, rinv * obs_values[...]], axis=1)
    sums = sum(dot16(placing, piece) for piece in split3(payload))
    for o in range(slabs):
        for t in range(tiles):
            at = (o * tiles + t) * rows
            obs_out[o, 0, :, t * PROF : (t + 1) * PROF] = sums[at : at + rows, :PROF]
            obs_out[o, 1, :, t * PROF : (t + 1) * PROF] = sums[at : at + rows, PROF:]
    loads[5].wait()
    for m in range(held):
        edge_out[0, m : m + 1, :] = state[m, 0:1, :]
        edge_out[1, m : m + 1, :] = state[m, rows - 1 : rows, :]

    for load in loads[6:]:
        load.wait()

    pl.semaphore_wait(barrier, group + slabs - 2)

    def edges(step, act):
        south, north = 2 * step, 2 * step + 1

        @pl.when(me_slab > 0)
        def _():
            act(south, north, me_slab - 1, 0)

        @pl.when(me_slab < slabs - 1)
        def _():
            act(north, south, me_slab + 1, 1)

    def edge_copy(mine, theirs, slab):
        return remote(
            edge_out.at[mine],
            edge_in.at[theirs],
            edge_send.at[mine],
            edge_recv.at[theirs],
            slab,
            me,
        )

    def edge_arrived(mine, slab):
        return remote(
            edge_out.at[mine],
            edge_in.at[mine],
            edge_send.at[mine],
            edge_recv.at[mine],
            slab,
            me,
        )

    def coefficients(row, side, at):
        sign = 0.5 if side == 0 else -0.5
        return sign * winds[1, row : row + 1, at] + kappa[row : row + 1, at]

    def advance(load, store):
        def body(c, carry):
            advance_at(load, store, c)
            return carry

        lax.fori_loop(0, group, body, 0)

    def advance_at(load, store, c):
        at = pl.multiple_of(c * width, PROF)
        before = pl.multiple_of(lax.rem(c * width + lon - PROF, lon), PROF)
        after = pl.multiple_of(lax.rem(c * width + width, lon), PROF)
        east_wind = 0.5 * winds[0, :, pl.ds(at, width)]
        north_wind = 0.5 * winds[1, :, pl.ds(at, width)]
        mix = kappa[:, pl.ds(at, width)]
        row = iota((rows, width), 0)
        for m in range(held):
            cell = load[m, :, pl.ds(at, width)]
            wide = jnp.concatenate(
                [load[m, :, pl.ds(before, PROF)], cell, load[m, :, pl.ds(after, PROF)]], axis=1
            )
            east = pltpu.roll(wide, width + 2 * PROF - 1, 1)[:, PROF : PROF + width]
            west = pltpu.roll(wide, 1, 1)[:, PROF : PROF + width]
            north = jnp.where(row == rows - 1, 0.0, pltpu.roll(cell, rows - 1, 0))
            south = jnp.where(row == 0, 0.0, pltpu.roll(cell, 1, 0))
            store(
                c,
                at,
                m,
                cell
                - east_wind * (east - west)
                - north_wind * (north - south)
                + mix * (east + west + north + south - 4.0 * cell),
            )

    edges(0, lambda mine, theirs, slab, side: edge_copy(mine, theirs, slab).start())

    def obs_copy(k, half):
        return remote(
            obs_out.at[peer_slab(k), half],
            obs_in.at[me_slab, half],
            obs_send.at[2 * k + half],
            obs_recv.at[2 * k + half],
            peer_slab(k),
            me,
        )

    for k in range(1, slabs):
        obs_copy(k, 0).start()

    def store_first(c, at, m, value):
        first[m, :, pl.ds(at, width)] = value

    advance(state, store_first)

    inner = rows - 4
    bulk = held * inner

    def store_inner(c, at, m, value):
        fields[c, m * inner : (m + 1) * inner, :] = value[2 : rows - 2]

    def inner_copy(k):
        return remote(
            fields.at[peer(k), 0:bulk],
            seen.at[me, 0:bulk],
            field_send.at[k],
            field_recv.at[k],
            me_slab,
            peer(k),
        )

    def send_inner(k, carry):
        advance_at(first, store_inner, peer(k))
        inner_copy(k).start()
        return carry

    lax.fori_loop(1, group, send_inner, 0)
    advance_at(first, store_inner, me)

    def mend_first(mine, theirs, slab, side):
        edge_arrived(mine, slab).wait_recv()
        row = 0 if side == 0 else rows - 1
        gain = coefficients(row, side, slice(None))
        for m in range(held):
            first[m, row : row + 1, :] += gain * edge_in[mine, m : m + 1, :]

    edges(0, mend_first)
    for m in range(held):
        edge_out[2, m : m + 1, :] = first[m, 0:1, :]
        edge_out[3, m : m + 1, :] = first[m, rows - 1 : rows, :]
    edges(1, lambda mine, theirs, slab, side: edge_copy(mine, theirs, slab).start())

    for k in range(1, slabs):
        obs_copy(k, 1).start()

    def store_rim(c, at, m, value):
        row = bulk + 4 * m
        fields[c, row : row + 2, :] = value[0:2]
        fields[c, row + 2 : row + 4, :] = value[rows - 2 : rows]

    advance(first, store_rim)

    def mend_second(mine, theirs, slab, side):
        edge_arrived(mine, slab).wait_recv()
        row = 0 if side == 0 else rows - 1
        for c in range(group):
            at = slice(c * width, (c + 1) * width)
            gain = coefficients(row, side, at)
            for m in range(held):
                place = bulk + 4 * m + 3 * side
                fields[c, place : place + 1, :] += gain * edge_in[mine, m : m + 1, at]

    edges(1, mend_second)

    def rim_copy(k):
        return remote(
            fields.at[peer(k), bulk : held * rows],
            seen.at[me, bulk : held * rows],
            field_send.at[group + k],
            field_recv.at[group + k],
            me_slab,
            peer(k),
        )

    for k in range(1, group):
        rim_copy(k).start()
    seen[me] = fields[me]

    for t in range(tiles):
        a, b = iota((span, lanes), 0), iota((span, lanes), 1)
        gather_sel[t * span : (t + 1) * span, :] = (b == t * members + a // rows).astype(
            jnp.bfloat16
        )
    use = jnp.maximum(
        tile_mask[0].astype(jnp.float32),
        (iota((all_tiles, all_tiles), 0) == iota((all_tiles, all_tiles), 1)).astype(jnp.float32),
    ).astype(jnp.bfloat16)
    lane = iota((1, lanes), 1)
    is_gram = lane < packed
    tile_lane = jnp.where(is_gram, lane // members, lane - packed)
    tile_lane = jnp.where(lane < packed + tiles, tile_lane, -1)
    column_lane = jnp.where(is_gram, lax.rem(lane, members), members)
    mine_sel = (
        (iota((all_tiles, lanes), 0) == me * tiles + tile_lane) & (tile_lane >= 0)
    ).astype(jnp.bfloat16)
    use_lane = dot16(use, mine_sel, ((0,), (0,))).astype(jnp.bfloat16)
    sub = iota((lanes, 1), 0)
    sub_gram = sub < packed
    tile_sub = jnp.where(sub_gram, sub // members, sub - packed)
    column_sub = jnp.where(sub_gram, lax.rem(sub, members), members)
    tile_sub = jnp.where(sub < packed + tiles, tile_sub, -all_tiles)
    same_column = (column_lane == column_sub).astype(jnp.float32)
    for d in range(group):
        pick = (iota((lanes, all_tiles), 1) == d * tiles + tile_sub).astype(jnp.bfloat16)
        use_sel[d * lanes : (d + 1) * lanes, :] = (dot16(pick, use_lane) * same_column).astype(
            jnp.bfloat16
        )

    weight, value = obs_out[me_slab, 0], obs_out[me_slab, 1]
    for k in range(1, slabs):
        s = source_slab(k)
        for half in range(2):
            n = 2 * k + half
            remote(
                obs_in.at[s, half], obs_in.at[s, half], obs_send.at[n], obs_recv.at[n], s, me
            ).wait_recv()
        weight = weight + obs_in[s, 0]
        value = value + obs_in[s, 1]

    for k in range(1, group):
        s = source(k)
        for n, at in ((k, slice(0, bulk)), (group + k, slice(bulk, held * rows))):
            remote(
                seen.at[s, at], seen.at[s, at], field_send.at[n], field_recv.at[n], me_slab, s
            ).wait_recv()

    def field(e):
        d, m = e // held, e % held
        rim = bulk + 4 * m
        return jnp.concatenate(
            [
                seen[d, rim : rim + 2, :],
                seen[d, m * inner : (m + 1) * inner, :],
                seen[d, rim + 2 : rim + 4, :],
            ],
            axis=0,
        )

    total = jnp.zeros((rows, width), jnp.float32)
    for e in range(members):
        cell = field(e)
        ordered[e] = cell
        total = total + cell
    mean = total * (1.0 / members)
    mean_ref[...] = mean
    missing = value - weight * mean
    for e in range(members):
        at = slice(e * rows, (e + 1) * rows)
        dev = ordered[e] - mean
        dev_high[at, :], dev_low[at, :] = split2(dev)
        weighted_high[at, :], weighted_low[at, :] = split2(dev * weight)
        innov_rows[e : e + 1, :] = jnp.sum(dev * missing, axis=0, keepdims=True)

    same_row = lax.rem(iota((span, span), 0), rows) == lax.rem(iota((span, span), 1), rows)
    diagonals = []
    for t in range(tiles):
        at = slice(t * PROF, (t + 1) * PROF)
        high = dev_high[:, at]
        gram = dot16(
            jnp.concatenate([weighted_high[:, at], weighted_low[:, at]], axis=1),
            jnp.concatenate([high, high], axis=1),
            ((1,), (1,)),
        ) + dot16(weighted_high[:, at], dev_low[:, at], ((1,), (1,)))
        gram = jnp.where(same_row, gram, 0.0)
        diagonals.append(jnp.sum(gram.reshape(members, rows, span), axis=1))
    packed_part = exact_rows(jnp.concatenate(diagonals, axis=1), gather_sel[...])
    for t in range(tiles):
        innov = jnp.sum(innov_rows[:, t * PROF : (t + 1) * PROF], axis=1, keepdims=True)
        packed_part = packed_part + jnp.where(lane == packed + t, innov, 0.0)
    part[...] = packed_part

    def part_copy(k):
        return remote(
            part, parts.at[me], part_send.at[k], part_recv.at[k], me_slab, peer(k)
        )

    for k in range(1, group):
        part_copy(k).start()
    parts[me] = packed_part
    for k in range(1, group):
        s = source(k)
        remote(
            parts.at[s], parts.at[s], part_send.at[k], part_recv.at[k], me_slab, s
        ).wait_recv()
    sums = exact_rows(jnp.concatenate([parts[d] for d in range(group)], axis=1), use_sel[...])

    a, b = iota((packed, packed), 0), iota((packed, packed), 1)
    same_tile = (a // members) == (b // members)
    identity = (a == b).astype(jnp.float32)
    matrix = jnp.where(
        same_tile, jnp.concatenate([sums[:, :packed]] * tiles, axis=0), 0.0
    ) + (members - 1.0) * identity
    row_sum = jnp.sum(matrix * matrix, axis=1, keepdims=True)
    tile_of = iota((packed, 1), 0) // members
    square = jnp.zeros((packed, 1), jnp.float32)
    for t in range(tiles):
        here = jnp.sum(row_sum[t * members : (t + 1) * members], axis=0, keepdims=True)
        square = jnp.where(tile_of == t, here, square)
    frob = jnp.sqrt(square + 1e-06)
    iterate = matrix / frob
    middle = 1.5 * identity - 0.5 * iterate
    factor = middle
    iterate = dot32(iterate, middle)
    for step in range(1, NS_ITERS):
        middle = 1.5 * identity - 0.5 * dot32(factor, iterate)
        if step < NS_ITERS - 1:
            iterate = dot32(iterate, middle)
        factor = dot32(middle, factor)
    inv_root = factor / jnp.sqrt(frob)
    innov = jnp.concatenate([sums[:, packed + t : packed + t + 1] for t in range(tiles)], axis=0)
    shift = dot32(inv_root, dot32(inv_root, jnp.broadcast_to(innov, (packed, packed))))
    mixing = jnp.where(same_tile, shift + math.sqrt(members - 1.0) * inv_root, 0.0)

    spread_sel = (
        lax.rem(iota((packed, span), 0), members) == iota((packed, span), 1) // rows
    ).astype(jnp.bfloat16)
    mix_high, mix_low = split2(mixing)
    spread_high = dot16(mix_high, spread_sel, ((0,), (0,)))
    spread_low = dot16(mix_low, spread_sel, ((0,), (0,)))
    mean = mean_ref[...]
    for t in range(tiles):
        at = slice(t * PROF, (t + 1) * PROF)

        def grow(spread):
            block = spread[t * members : (t + 1) * members]
            tall = jnp.broadcast_to(block[:, None, :], (members, rows, span)).reshape(span, span)
            return jnp.where(same_row, tall, 0.0).astype(jnp.bfloat16)

        high, low = dev_high[:, at], dev_low[:, at]
        both = dot16(grow(spread_high), jnp.concatenate([high, low], axis=1))
        update = both[:, :PROF] + both[:, PROF:] + dot16(grow(spread_low), high)
        update = update.reshape(members, rows, PROF) + mean[None, :, at]
        for e in range(members):
            result[e // held, e % held, :, at] = update[e]

    columns = pl.ds(pl.multiple_of(me * width, PROF), width)

    def back_copy(k):
        return remote(
            result.at[peer(k)],
            out.at[:, :, columns],
            back_send.at[k],
            back_recv.at[k],
            me_slab,
            peer(k),
        )

    for k in range(1, group):
        back_copy(k).start()
    own = pltpu.make_async_copy(result.at[me], out.at[:, :, columns], own_sem)
    own.start()
    edges(0, lambda mine, theirs, slab, side: edge_copy(mine, theirs, slab).wait_send())
    edges(1, lambda mine, theirs, slab, side: edge_copy(mine, theirs, slab).wait_send())
    for k in range(1, slabs):
        obs_copy(k, 0).wait_send()
        obs_copy(k, 1).wait_send()
    for k in range(1, group):
        inner_copy(k).wait_send()
        rim_copy(k).wait_send()
        part_copy(k).wait_send()
    for k in range(1, group):
        s = source(k)
        theirs = pl.ds(pl.multiple_of(s * width, PROF), width)
        back_copy(k).wait_send()
        remote(
            result.at[s], out.at[:, :, theirs], back_send.at[k], back_recv.at[k], me_slab, s
        ).wait_recv()
    own.wait()


def in_one_kernel(
    state, winds, kappa, obs_values, obs_rinv, owner, obs_rows, obs_tiles, counts, tile_mask
):
    slabs, group = lax.axis_size("slab"), lax.axis_size("member")
    held, rows, lon = state.shape
    width = lon // group
    tiles = width // PROF
    members = held * group
    span = members * rows
    packed = tiles * members
    lanes = -(-(packed + tiles) // 128) * 128
    f32, bf16 = jnp.float32, jnp.bfloat16
    dma = pltpu.SemaphoreType.DMA
    hbm = pl.BlockSpec(memory_space=pltpu.HBM)
    return pl.pallas_call(
        functools.partial(kernel, slabs, group),
        out_shape=jax.ShapeDtypeStruct(state.shape, f32),
        in_specs=[hbm] * 8 + [pl.BlockSpec(memory_space=pltpu.SMEM), hbm],
        out_specs=pl.BlockSpec(memory_space=pl.ANY),
        scratch_shapes=[
            pltpu.VMEM(state.shape, f32),
            pltpu.VMEM(winds.shape, f32),
            pltpu.VMEM(kappa.shape, f32),
            pltpu.VMEM(obs_values.shape, f32),
            pltpu.VMEM(obs_rinv.shape, f32),
            pltpu.VMEM((1, owner.shape[0]), jnp.int32),
            pltpu.VMEM((1, owner.shape[0]), jnp.int32),
            pltpu.VMEM((1, owner.shape[0]), jnp.int32),
            pltpu.VMEM(tile_mask.shape, jnp.int32),
            dma((9,)),
            pltpu.VMEM((held, rows, lon), f32),
            pltpu.VMEM((group, held * rows, width), f32),
            pltpu.VMEM((4, held, lon), f32),
            pltpu.VMEM((4, held, lon), f32),
            pltpu.VMEM((slabs, 2, rows, width), f32),
            pltpu.VMEM((slabs, 2, rows, width), f32),
            pltpu.VMEM((group, held * rows, width), f32),
            pltpu.VMEM((members, rows, width), f32),
            pltpu.VMEM((members, lanes), f32),
            pltpu.VMEM((group, members, lanes), f32),
            pltpu.VMEM((span, width), bf16),
            pltpu.VMEM((span, width), bf16),
            pltpu.VMEM((span, width), bf16),
            pltpu.VMEM((span, width), bf16),
            pltpu.VMEM((members, width), f32),
            pltpu.VMEM((rows, width), f32),
            pltpu.VMEM((tiles * span, lanes), bf16),
            pltpu.VMEM((group * lanes, lanes), bf16),
            pltpu.VMEM((group, held, rows, width), f32),
            dma((4,)),
            dma((4,)),
            dma((2 * slabs,)),
            dma((2 * slabs,)),
            dma((2 * group,)),
            dma((2 * group,)),
            dma((group,)),
            dma((group,)),
            dma((group,)),
            dma((group,)),
            dma,
        ],
        compiler_params=pltpu.CompilerParams(
            collective_id=0, has_side_effects=True, vmem_limit_bytes=40 * 2**20
        ),
    )(
        *(
            pltpu.with_memory_space_constraint(x, pltpu.HBM)
            for x in (
                state,
                winds,
                kappa,
                obs_values,
                obs_rinv,
                owner[:, 0][None, :],
                obs_rows[None, :],
                obs_tiles[None, :],
            )
        ),
        counts,
        pltpu.with_memory_space_constraint(tile_mask, pltpu.HBM),
    )


def per_device(state, winds, *rest):
    held, rows = state.shape[:2]
    spare = held * (rows - 4) % 8
    if held * lax.axis_size("member") * rows <= 256 and spare == 0:
        return in_one_kernel(state, winds, *rest)
    return on_device(state, winds, *rest)


def solution(mesh):
    placed = (
        P("member", "slab", None),
        P(None, "slab", None),
        P("slab", None),
        P("slab", None),
        P("slab", None),
        P("slab", None),
        P("slab"),
        P("slab"),
        P("slab"),
        P("slab", None, None),
    )
    return jax.shard_map(
        per_device, mesh=mesh, in_specs=placed, out_specs=P("member", "slab", None), check_vma=False
    )
```
